32 devices in a mesh: groups: 2 (over x), row: 16 (over z, y, core).
Axes of the slice: x: 2, y: 2, z: 4, core: 2. Of those that a mesh axis runs over, the one named last changes fastest.
Arguments:
- left_proj: bfloat16 [128, 8192], P('groups', 'row'), parts along dimension 0, may hold values from -6 to 6
- right_proj: bfloat16 [128, 8192], P('groups', 'row'), parts along dimension 0, may hold values from -6 to 6
- pair_cot: bfloat16 [512, 256, 128], P(('groups', 'row')), parts along dimension 0, may hold values from -6 to 6
- out_weight: bfloat16 [1024, 128], replicated, may hold values from -0.1875 to 0.1875
Outputs:
- grad_left: bfloat16 [128, 8192], P('groups', 'row'), parts along dimension 0
- grad_right: bfloat16 [128, 8192], P('groups', 'row'), parts along dimension 0
The draws below stay inside these ranges and needn't reach their ends.
There are 2 independent parts, one for each index of `groups`. The reference program is written for one: setup_inputs(seed, part) draws one part's arguments, and reference() takes and returns one part's arrays. A program takes and returns all parts, laid end to end along the dimension named above; an argument that names none is the same for every part. Nothing has to cross between parts.
All inputs are finite; a program needn't handle non-finite values.
Results may differ from the reference program's by a relative error of at most 0.005.
Values may be sent and summed in bfloat16 or wider, within the bound.
A program may use at most 128 MiB of HBM per device.

```python
import jax
import jax.numpy as jnp
from jax import lax

C = 32
P_SIZE = 128
S = 64
R = 256


def levels(own_key, extent, cuts, least, top_value):
    def one(dim, shards_of):
        steps = jax.random.uniform(jax.random.fold_in(jax.random.fold_in(own_key, 6), dim), (shards_of,), jnp.float32, least / len(cuts), top_value / len(cuts))
        return jnp.repeat(jnp.exp(steps), extent[dim] // shards_of).reshape((-1,) + (1,) * (len(extent) - dim - 1))

    gain = one(*cuts[0])
    for cut in cuts[1:]:
        gain = gain * one(*cut)
    return gain


def normal_values(key, extent, width, bound, shards=(), dtype=jnp.bfloat16):
    loudness = levels(key, extent, shards, -0.22, 0.18) if shards else 1.0
    entries = jax.random.normal(key, extent, jnp.float32) * width * loudness
    return jnp.minimum(jnp.maximum(entries, -bound), bound).astype(dtype)


def setup_inputs(seed: int = 0, part: int = 0) -> dict:
    key_of = jax.random.split(jax.random.key(seed), 5)
    own_keys = jax.random.split(jax.random.fold_in(key_of[4], part), 5)
    return {
        "left_proj": normal_values(own_keys[0], (S, R * C), 1.0, 6.0, ((1, 16),)),
        "right_proj": normal_values(own_keys[1], (S, R * C), 1.0, 6.0, ((1, 16),)),
        "pair_cot": normal_values(own_keys[2], (R, R, P_SIZE), 1.0, 6.0, ((0, 16),)),
        "out_weight": normal_values(key_of[3], (C * C, P_SIZE), (C * C) ** -0.5, 0.1875),
    }


def reference(left_proj, right_proj, pair_cot, out_weight):
    n_seq = left_proj.shape[0]
    total = pair_cot.shape[0]
    block = 16
    left = left_proj.reshape(n_seq, total, C).astype(jnp.float32)
    right = right_proj.reshape(n_seq, total, C).astype(jnp.float32)
    cot_blocks = pair_cot.reshape(total // block, block, total, P_SIZE)
    left_blocks = left.reshape(n_seq, total // block, block, C).transpose(1, 0, 2, 3)

    def step(carry, inputs):
        slab, left_blk = inputs
        prod = jnp.dot(slab.reshape(-1, P_SIZE), out_weight.T, preferred_element_type=jnp.float32)
        grad = (prod / n_seq).astype(jnp.bfloat16).astype(jnp.float32).reshape(block, total, C, C)
        row_grad = jnp.einsum('ijce,sje->sic', grad, right)
        carry = carry + jnp.einsum('ijce,sic->sje', grad, left_blk)
        return carry, row_grad

    start = jnp.zeros((n_seq, total, C), jnp.float32)
    partial_sum, row_grads = lax.scan(step, start, (cot_blocks, left_blocks))
    grad_left = row_grads.transpose(1, 0, 2, 3).reshape(n_seq, total * C).astype(jnp.bfloat16)
    grad_right = partial_sum.reshape(n_seq, total * C).astype(jnp.bfloat16)
    return grad_left, grad_right
```

```python
import functools

import jax
import jax.numpy as jnp
from jax import lax
from jax.experimental import pallas as pl
from jax.experimental.pallas import tpu as pltpu
from jax.sharding import PartitionSpec as P

C = 32
CORES = 2
COLS = 2
HALF = C // 2
GROUPS = 4
MESH = pl.DeviceIdType.MESH
F32 = jnp.float32
BF16 = jnp.bfloat16


def kernel(
    depth, n_seq, block,
    left_ref, right_ref, pair_ref, weight_ref,
    out_left, out_right,
    pair_own, pair_sib, left_sib, weight_f32, weight_perm, grad, rows_f32,
    gathered, right_all, column_sum, y_send, y_recv, z_send, z_recv, total,
    left_acc, left_send, left_recv,
    load_sem, sib_send, sib_recv, agz_send, agz_recv, agy_send, agy_recv,
    rsy_send, rsy_recv, rsz_send, rsz_recv,
):
    me = lax.axis_index("row")
    core = lax.rem(me, CORES)
    col = lax.rem(me // CORES, COLS)
    z = me // (CORES * COLS)
    sibling = me + 1 - 2 * core
    across = me + CORES * (1 - 2 * col)
    span = depth * block
    width = COLS * span
    chans = block * C
    lanes = 2 * n_seq
    per_group = HALF // GROUPS
    group_lanes = per_group * lanes

    def z_peer(step):
        return lax.rem(z + step, depth)

    def at_z(other):
        return other * (CORES * COLS) + lax.rem(me, CORES * COLS)

    def send(src, dst, s_sem, r_sem, target):
        return pltpu.make_async_remote_copy(
            src_ref=src, dst_ref=dst, send_sem=s_sem, recv_sem=r_sem,
            device_id={"row": target}, device_id_type=MESH,
        )

    barrier = pltpu.get_barrier_semaphore()
    for target in [sibling, across] + [at_z(z_peer(d)) for d in range(1, depth)]:
        pl.semaphore_signal(barrier, inc=1, device_id={"row": target}, device_id_type=MESH)

    loads = []
    for rel in range(COLS):
        which = col if rel == 0 else 1 - col
        loads.append(pltpu.make_async_copy(
            pair_ref.at[:, :, which, core], pair_own.at[:, rel], load_sem.at[rel]))
        loads[-1].start()

    wide = right_ref[...].astype(F32)
    rows_f32[...] = jnp.concatenate([wide, wide], axis=0).T
    low = lax.broadcasted_iota(jnp.int32, (block, lanes), 1) < n_seq
    for ep in range(HALF):
        even = rows_f32[pl.ds(2 * ep, block, stride=C), :]
        odd = rows_f32[pl.ds(2 * ep + 1, block, stride=C), :]
        gathered[ep, 0, z] = jnp.where(low, even, odd).astype(BF16)

    pl.semaphore_wait(barrier, depth + 1)

    sib = []
    for rel in range(COLS):
        which = col if rel == 0 else 1 - col
        sib.append(send(pair_ref.at[:, :, which, 1 - core], pair_sib.at[:, rel],
                        sib_send.at[rel], sib_recv.at[rel], sibling))
    sib.append(send(left_ref, left_sib, sib_send.at[2], sib_recv.at[2], sibling))
    gather_z = [
        send(gathered.at[:, 0, z], gathered.at[:, 0, z], agz_send.at[d - 1], agz_recv.at[d - 1],
             at_z(z_peer(d)))
        for d in range(1, depth)
    ]
    gather_y = []
    for d in range(depth):
        other = z if d == 0 else lax.rem(z + depth - d, depth)
        gather_y.append(send(gathered.at[:, 0, other], gathered.at[:, 1, other],
                             agy_send.at[d], agy_recv.at[d], across))
    for copy in gather_z:
        copy.start()
    for copy in sib:
        copy.start()
    gather_y[0].start()

    weight_f32[...] = weight_ref[...].astype(F32)
    for e in range(C):
        weight_perm[e * C:(e + 1) * C, :] = weight_f32[pl.ds(e, C, stride=C), :].astype(BF16)

    def project(pair, first):
        def step(t, carry):
            slab = pair[pl.ds(2 * t, 2)].reshape(2 * width, -1)
            res = lax.dot_general(weight_perm[...], slab, (((1,), (1,)), ((), ())),
                                  preferred_element_type=F32).astype(BF16)
            for k in range(2):
                row = pl.multiple_of(first + (2 * t + k) * C, C)
                for e in range(C):
                    grad[pl.ds(row, C), e * width:(e + 1) * width] = (
                        res[e * C:(e + 1) * C, k * width:(k + 1) * width])
            return carry

        lax.fori_loop(0, block // 2, step, 0)

    for copy in loads:
        copy.wait()
    project(pair_own, 0)
    for d in range(1, depth):
        gather_z[d - 1].wait_recv()
        gather_y[d].start()
    for copy in sib:
        copy.wait_recv()
    project(pair_sib, chans)

    reduce_y = [send(y_send.at[g], y_recv.at[g], rsy_send.at[g], rsy_recv.at[g], across)
                for g in range(GROUPS)]
    reduce_z = [
        [send(z_send.at[g, z_peer(d)], z_recv.at[g, d - 1],
              rsz_send.at[g, d - 1], rsz_recv.at[g, d - 1], at_z(z_peer(d)))
         for d in range(1, depth)]
        for g in range(GROUPS)
    ]

    def columns(g):
        for q in range(per_group):
            ep = g * per_group + q
            part = slice(2 * ep * width, 2 * (ep + 1) * width)
            res = jnp.dot(left_ref[...], grad[:chans, part], preferred_element_type=F32)
            res += jnp.dot(left_sib[...], grad[chans:, part], preferred_element_type=F32)
            turned = jnp.concatenate([res[:, :width], res[:, width:]], axis=0).T
            where = slice(q * lanes, (q + 1) * lanes)
            column_sum[g, :, where] = turned[:span]
            y_send[g, :, where] = turned[span:].astype(BF16)
        reduce_y[g].start()

    def second(g):
        reduce_y[g].wait_recv()
        column_sum[g] += y_recv[g].astype(F32)
        for k in range(depth):
            z_send[g, k] = column_sum[g, k * block:(k + 1) * block, :].astype(BF16)
        for copy in reduce_z[g]:
            copy.start()

    def rows(first):
        left_acc[...] = jnp.zeros_like(left_acc)

        def step(ep, carry):
            at = pl.multiple_of(ep * 2 * width, 2 * width)
            left_acc[...] += jnp.dot(grad[first:first + chans, pl.ds(at, 2 * width)],
                                     right_all[pl.ds(at, 2 * width), :],
                                     preferred_element_type=F32)
            return carry

        lax.fori_loop(0, HALF, step, 0)
        turned = left_acc[...].T
        return turned[:n_seq] + turned[n_seq:]

    columns(0)
    columns(1)
    columns(2)
    second(0)
    columns(3)
    second(1)

    for copy in gather_y:
        copy.wait_recv()
    upper = lax.broadcasted_iota(jnp.int32, (width, lanes), 1) >= n_seq
    mask_odd = upper.astype(F32).astype(BF16)
    mask_even = (1.0 - upper.astype(F32)).astype(BF16)
    for ep in range(HALF):
        piece = gathered[ep].reshape(width, lanes)
        right_all[2 * ep * width:(2 * ep + 1) * width, :] = piece * mask_even
        right_all[(2 * ep + 1) * width:(2 * ep + 2) * width, :] = piece * mask_odd

    second(2)
    left_send[...] = rows(chans)
    exchange = send(left_send, left_recv, sib_send.at[3], sib_recv.at[3], sibling)
    exchange.start()
    second(3)
    mine = rows(0)
    exchange.wait_recv()
    out_left[...] = ((mine + left_recv[...]) * (1.0 / n_seq)).astype(BF16)

    for g in range(GROUPS):
        acc = column_sum[g, pl.ds(pl.multiple_of(z * block, block), block), :]
        for d in range(1, depth):
            reduce_z[g][d - 1].wait_recv()
            acc += z_recv[g, d - 1].astype(F32)
        for q in range(per_group):
            ep = g * per_group + q
            tile = acc[:, q * lanes:(q + 1) * lanes] * (1.0 / n_seq)
            rows_f32[pl.ds(2 * ep, block, stride=C), :] = tile
            rows_f32[pl.ds(2 * ep + 1, block, stride=C), :] = pltpu.roll(tile, n_seq, 1)
    out_right[...] = rows_f32[...].T[:n_seq].astype(BF16)

    for copy in sib + gather_z + gather_y + reduce_y + [exchange]:
        copy.wait_send()
    for group in reduce_z:
        for copy in group:
            copy.wait_send()


def per_device(n_row, left_proj, right_proj, pair_cot, out_weight):
    n_seq = left_proj.shape[0]
    block, total, p_size = pair_cot.shape
    depth = n_row // (CORES * COLS)
    span = depth * block
    width = COLS * span
    chans = block * C
    lanes = 2 * n_seq
    group_lanes = HALF // GROUPS * lanes
    pair = pair_cot.reshape(block, depth, COLS, CORES, block, p_size)
    vmem = pl.BlockSpec(memory_space=pltpu.VMEM)
    dma = pltpu.SemaphoreType.DMA
    flops = 2 * block * total * C * C * (p_size + 2 * n_seq)
    return pl.pallas_call(
        functools.partial(kernel, depth, n_seq, block),
        out_shape=[jax.ShapeDtypeStruct((n_seq, chans), BF16)] * 2,
        in_specs=[vmem, vmem, pl.BlockSpec(memory_space=pl.ANY), vmem],
        out_specs=[vmem, vmem],
        scratch_shapes=[
            pltpu.VMEM((block, COLS, depth, block, p_size), BF16),
            pltpu.VMEM((block, COLS, depth, block, p_size), BF16),
            pltpu.VMEM((n_seq, chans), BF16),
            pltpu.VMEM((C * C, p_size), F32),
            pltpu.VMEM((C * C, p_size), BF16),
            pltpu.VMEM((2 * chans, C * width), BF16),
            pltpu.VMEM((chans, lanes), F32),
            pltpu.VMEM((HALF, COLS, depth, block, lanes), BF16),
            pltpu.VMEM((C * width, lanes), BF16),
            pltpu.VMEM((GROUPS, span, group_lanes), F32),
            pltpu.VMEM((GROUPS, span, group_lanes), BF16),
            pltpu.VMEM((GROUPS, span, group_lanes), BF16),
            pltpu.VMEM((GROUPS, depth, block, group_lanes), BF16),
            pltpu.VMEM((GROUPS, depth - 1, block, group_lanes), BF16),
            pltpu.VMEM((8, 128), F32),
            pltpu.VMEM((chans, lanes), F32),
            pltpu.VMEM((n_seq, chans), F32),
            pltpu.VMEM((n_seq, chans), F32),
            dma((COLS,)),
            dma((4,)), dma((4,)),
            dma((depth - 1,)), dma((depth - 1,)),
            dma((depth,)), dma((depth,)),
            dma((GROUPS,)), dma((GROUPS,)),
            dma((GROUPS, depth - 1)), dma((GROUPS, depth - 1)),
        ],
        compiler_params=pltpu.CompilerParams(
            collective_id=0, has_side_effects=True, vmem_limit_bytes=60 * 1024 * 1024
        ),
        cost_estimate=pl.CostEstimate(
            flops=flops, bytes_accessed=4 * pair_cot.size, transcendentals=0
        ),
    )(left_proj, right_proj, pair, out_weight)


def solution(mesh):
    return jax.shard_map(
        functools.partial(per_device, mesh.shape["row"]),
        mesh=mesh,
        in_specs=(P("groups", "row"), P("groups", "row"), P(("groups", "row"), None, None), P()),
        out_specs=(P("groups", "row"), P("groups", "row")),
        check_vma=False,
    )
```

```python
import functools

import jax
import jax.numpy as jnp
from jax import lax
from jax.experimental import pallas as pl
from jax.experimental.pallas import tpu as pltpu
from jax.sharding import PartitionSpec as P

C = 32
CORES = 2
COLS = 2
HALF = C // 2
GROUPS = 4
MESH = pl.DeviceIdType.MESH
F32 = jnp.float32
BF16 = jnp.bfloat16


def kernel(
    depth, n_seq, block,
    left_ref, right_ref, pair_ref, weight_ref,
    out,
    pair_own, pair_sib, left_sib, weight_f32, weight_perm, grad, rows_f32,
    gathered, right_all, column_sum, y_send, y_recv, z_send, z_recv,
    left_send, left_recv,
    load_sem, sib_send, sib_recv, agz_send, agz_recv, agy_send, agy_recv,
    rsy_send, rsy_recv, rsz_send, rsz_recv,
):
    me = lax.axis_index("row")
    core = lax.rem(me, CORES)
    col = lax.rem(me // CORES, COLS)
    z = me // (CORES * COLS)
    sibling = me + 1 - 2 * core
    across = me + CORES * (1 - 2 * col)
    span = depth * block
    width = COLS * span
    chans = block * C
    lanes = 2 * n_seq
    per_group = HALF // GROUPS
    group_lanes = per_group * lanes

    def z_peer(step):
        return lax.rem(z + step, depth)

    def at_z(other):
        return other * (CORES * COLS) + lax.rem(me, CORES * COLS)

    def send(src, dst, s_sem, r_sem, target):
        return pltpu.make_async_remote_copy(
            src_ref=src, dst_ref=dst, send_sem=s_sem, recv_sem=r_sem,
            device_id={"row": target}, device_id_type=MESH,
        )

    barrier = pltpu.get_barrier_semaphore()
    for target in [sibling, across] + [at_z(z_peer(d)) for d in range(1, depth)]:
        pl.semaphore_signal(barrier, inc=1, device_id={"row": target}, device_id_type=MESH)

    loads = []
    for rel in range(COLS):
        which = col if rel == 0 else 1 - col
        loads.append(pltpu.make_async_copy(
            pair_ref.at[:, :, which, core], pair_own.at[:, rel], load_sem.at[rel]))
        loads[-1].start()

    wide = right_ref[...].astype(F32)
    rows_f32[...] = jnp.concatenate([wide, wide], axis=0).T
    low = lax.broadcasted_iota(jnp.int32, (block, lanes), 1) < n_seq
    for ep in range(HALF):
        even = rows_f32[pl.ds(2 * ep, block, stride=C), :]
        odd = rows_f32[pl.ds(2 * ep + 1, block, stride=C), :]
        gathered[ep, 0, z] = jnp.where(low, even, odd).astype(BF16)

    pl.semaphore_wait(barrier, depth + 1)

    sib = []
    for rel in range(COLS):
        which = col if rel == 0 else 1 - col
        sib.append(send(pair_ref.at[:, :, which, 1 - core], pair_sib.at[:, rel],
                        sib_send.at[rel], sib_recv.at[rel], sibling))
    sib.append(send(left_ref, left_sib, sib_send.at[2], sib_recv.at[2], sibling))
    gather_z = [
        send(gathered.at[:, 0, z], gathered.at[:, 0, z], agz_send.at[d - 1], agz_recv.at[d - 1],
             at_z(z_peer(d)))
        for d in range(1, depth)
    ]
    gather_y = []
    for d in range(depth):
        other = z if d == 0 else lax.rem(z + depth - d, depth)
        gather_y.append(send(gathered.at[:, 0, other], gathered.at[:, 1, other],
                             agy_send.at[d], agy_recv.at[d], across))
    for copy in gather_z:
        copy.start()
    for copy in sib:
        copy.start()
    gather_y[0].start()

    weight_f32[...] = weight_ref[...].astype(F32)
    for e in range(C):
        weight_perm[e * C:(e + 1) * C, :] = weight_f32[pl.ds(e, C, stride=C), :].astype(BF16)

    rows_g = C // GROUPS * C

    def project(g, pair, first):
        taps = weight_perm[g * rows_g:(g + 1) * rows_g, :]

        def step(t, carry):
            slab = pair[pl.ds(2 * t, 2)].reshape(2 * width, -1)
            res = lax.dot_general(taps, slab, (((1,), (1,)), ((), ())),
                                  preferred_element_type=F32).astype(BF16)
            for k in range(2):
                row = pl.multiple_of(first + (2 * t + k) * C, C)
                for q in range(C // GROUPS):
                    e = g * (C // GROUPS) + q
                    grad[pl.ds(row, C), e * width:(e + 1) * width] = (
                        res[q * C:(q + 1) * C, k * width:(k + 1) * width])
            return carry

        lax.fori_loop(0, block // 2, step, 0, unroll=4)

    reduce_y = [send(y_send.at[g], y_recv.at[g], rsy_send.at[g], rsy_recv.at[g], across)
                for g in range(GROUPS)]
    reduce_z = [
        [send(z_send.at[g, z_peer(d)], z_recv.at[g, d - 1],
              rsz_send.at[g, d - 1], rsz_recv.at[g, d - 1], at_z(z_peer(d)))
         for d in range(1, depth)]
        for g in range(GROUPS)
    ]

    def columns(g):
        part = slice(g * per_group * 2 * width, (g + 1) * per_group * 2 * width)
        res = jnp.dot(left_ref[...], grad[:chans, part], preferred_element_type=F32)
        res += jnp.dot(left_sib[...], grad[chans:, part], preferred_element_type=F32)
        for q in range(per_group):
            at = 2 * q * width
            turned = jnp.concatenate(
                [res[:, at:at + width], res[:, at + width:at + 2 * width]], axis=0).T
            where = slice(q * lanes, (q + 1) * lanes)
            column_sum[g, :, where] = turned[:span]
            y_send[g, :, where] = turned[span:].astype(BF16)
        reduce_y[g].start()

    def second(g):
        reduce_y[g].wait_recv()
        column_sum[g] += y_recv[g].astype(F32)
        for k in range(depth):
            z_send[g, k] = column_sum[g, k * block:(k + 1) * block, :].astype(BF16)
        for copy in reduce_z[g]:
            copy.start()

    def rows(first):
        part = per_group * 2 * width
        acc = None
        for g in range(GROUPS):
            term = jnp.dot(grad[first:first + chans, g * part:(g + 1) * part],
                           right_all[g * part:(g + 1) * part, :], preferred_element_type=F32)
            acc = term if acc is None else acc + term
        turned = acc.T
        return turned[:n_seq] + turned[n_seq:]

    for copy in loads:
        copy.wait()
    for g in range(GROUPS):
        project(g, pair_own, 0)
        if g == 0:
            for copy in sib:
                copy.wait_recv()
        project(g, pair_sib, chans)
        for d in range(1, depth):
            if (d - 1) * (GROUPS - 1) // (depth - 1) == g - 1:
                gather_z[d - 1].wait_recv()
                gather_y[d].start()
        columns(g)
        if g >= 2:
            second(g - 2)

    for copy in gather_y:
        copy.wait_recv()
    upper = lax.broadcasted_iota(jnp.int32, (width, lanes), 1) >= n_seq
    mask_odd = upper.astype(F32).astype(BF16)
    mask_even = (1.0 - upper.astype(F32)).astype(BF16)
    for ep in range(HALF):
        piece = gathered[ep].reshape(width, lanes)
        right_all[2 * ep * width:(2 * ep + 1) * width, :] = piece * mask_even
        right_all[(2 * ep + 1) * width:(2 * ep + 2) * width, :] = piece * mask_odd

    second(2)
    left_send[...] = rows(chans)
    exchange = send(left_send, left_recv, sib_send.at[3], sib_recv.at[3], sibling)
    exchange.start()
    second(3)
    mine = rows(0)
    exchange.wait_recv()
    out[0] = ((mine + left_recv[...]) * (1.0 / n_seq)).astype(BF16)

    for g in range(GROUPS):
        acc = column_sum[g, pl.ds(pl.multiple_of(z * block, block), block), :]
        for d in range(1, depth):
            reduce_z[g][d - 1].wait_recv()
            acc += z_recv[g, d - 1].astype(F32)
        for q in range(per_group):
            ep = g * per_group + q
            tile = acc[:, q * lanes:(q + 1) * lanes] * (1.0 / n_seq)
            rows_f32[pl.ds(2 * ep, block, stride=C), :] = tile
            rows_f32[pl.ds(2 * ep + 1, block, stride=C), :] = pltpu.roll(tile, n_seq, 1)
    out[1] = rows_f32[...].T[:n_seq].astype(BF16)

    for copy in sib + gather_z + gather_y + reduce_y + [exchange]:
        copy.wait_send()
    for group in reduce_z:
        for copy in group:
            copy.wait_send()


def per_device(n_row, left_proj, right_proj, pair_cot, out_weight):
    n_seq = left_proj.shape[0]
    block, total, p_size = pair_cot.shape
    depth = n_row // (CORES * COLS)
    span = depth * block
    width = COLS * span
    chans = block * C
    lanes = 2 * n_seq
    group_lanes = HALF // GROUPS * lanes
    pair = pair_cot.reshape(block, depth, COLS, CORES, block, p_size)
    vmem = pl.BlockSpec(memory_space=pltpu.VMEM)
    dma = pltpu.SemaphoreType.DMA
    flops = 2 * block * total * C * C * (p_size + 2 * n_seq)
    sums = pl.pallas_call(
        functools.partial(kernel, depth, n_seq, block),
        out_shape=jax.ShapeDtypeStruct((2, n_seq, chans), BF16),
        in_specs=[vmem, vmem, pl.BlockSpec(memory_space=pl.ANY), vmem],
        out_specs=vmem,
        scratch_shapes=[
            pltpu.VMEM((block, COLS, depth, block, p_size), BF16),
            pltpu.VMEM((block, COLS, depth, block, p_size), BF16),
            pltpu.VMEM((n_seq, chans), BF16),
            pltpu.VMEM((C * C, p_size), F32),
            pltpu.VMEM((C * C, p_size), BF16),
            pltpu.VMEM((2 * chans, C * width), BF16),
            pltpu.VMEM((chans, lanes), F32),
            pltpu.VMEM((HALF, COLS, depth, block, lanes), BF16),
            pltpu.VMEM((C * width, lanes), BF16),
            pltpu.VMEM((GROUPS, span, group_lanes), F32),
            pltpu.VMEM((GROUPS, span, group_lanes), BF16),
            pltpu.VMEM((GROUPS, span, group_lanes), BF16),
            pltpu.VMEM((GROUPS, depth, block, group_lanes), BF16),
            pltpu.VMEM((GROUPS, depth - 1, block, group_lanes), BF16),
            pltpu.VMEM((n_seq, chans), F32),
            pltpu.VMEM((n_seq, chans), F32),
            dma((COLS,)),
            dma((4,)), dma((4,)),
            dma((depth - 1,)), dma((depth - 1,)),
            dma((depth,)), dma((depth,)),
            dma((GROUPS,)), dma((GROUPS,)),
            dma((GROUPS, depth - 1)), dma((GROUPS, depth - 1)),
        ],
        compiler_params=pltpu.CompilerParams(
            collective_id=0, has_side_effects=True, vmem_limit_bytes=60 * 1024 * 1024
        ),
        cost_estimate=pl.CostEstimate(
            flops=flops, bytes_accessed=4 * pair_cot.size, transcendentals=0
        ),
    )(left_proj, right_proj, pair, out_weight)
    return (sums[0], sums[1])


def solution(mesh):
    return jax.shard_map(
        functools.partial(per_device, mesh.shape["row"]),
        mesh=mesh,
        in_specs=(P("groups", "row"), P("groups", "row"), P(("groups", "row"), None, None), P()),
        out_specs=(P("groups", "row"), P("groups", "row")),
        check_vma=False,
    )
```

```python
import functools
import math

import jax
import jax.numpy as jnp
from jax import lax
from jax.experimental import pallas as pl
from jax.experimental.pallas import tpu as pltpu
from jax.sharding import PartitionSpec as P

C = 32
CORES = 2
COLS = 2
HALF = C // 2
GROUPS = 2
MESH = pl.DeviceIdType.MESH
F32 = jnp.float32
BF16 = jnp.bfloat16


def kernel(
    depth, n_seq, block,
    left_ref, right_ref, pair_ref, weight_ref,
    out,
    pair_own, pair_sib, left_sib, weight_f32, weight_perm, grad, rows_f32,
    gathered, right_all, column_sum, y_send, y_recv, z_send, z_recv,
    left_send, left_recv,
    load_sem, sib_send, sib_recv, agz_send, agz_recv, agy_send, agy_recv,
    rsy_send, rsy_recv, rsz_send, rsz_recv,
):
    me = lax.axis_index("row")
    core = lax.rem(me, CORES)
    col = lax.rem(me // CORES, COLS)
    z = me // (CORES * COLS)
    sibling = me + 1 - 2 * core
    across = me + CORES * (1 - 2 * col)
    span = depth * block
    width = COLS * span
    chans = block * C
    lanes = 2 * n_seq
    per_group = HALF // GROUPS
    group_lanes = per_group * lanes

    def z_peer(step):
        return lax.rem(z + step, depth)

    def at_z(other):
        return other * (CORES * COLS) + lax.rem(me, CORES * COLS)

    def send(src, dst, s_sem, r_sem, target):
        return pltpu.make_async_remote_copy(
            src_ref=src, dst_ref=dst, send_sem=s_sem, recv_sem=r_sem,
            device_id={"row": target}, device_id_type=MESH,
        )

    barrier = pltpu.get_barrier_semaphore()
    for target in [sibling, across] + [at_z(z_peer(d)) for d in range(1, depth)]:
        pl.semaphore_signal(barrier, inc=1, device_id={"row": target}, device_id_type=MESH)

    loads = []
    for rel in range(COLS):
        which = col if rel == 0 else 1 - col
        loads.append(pltpu.make_async_copy(
            pair_ref.at[:, :, which, core], pair_own.at[:, rel], load_sem.at[rel]))
        loads[-1].start()

    wide = right_ref[...].astype(F32)
    rows_f32[...] = jnp.concatenate([wide, wide], axis=0).T
    low = lax.broadcasted_iota(jnp.int32, (block, lanes), 1) < n_seq
    for ep in range(HALF):
        even = rows_f32[pl.ds(2 * ep, block, stride=C), :]
        odd = rows_f32[pl.ds(2 * ep + 1, block, stride=C), :]
        gathered[ep, 0, z] = jnp.where(low, even, odd).astype(BF16)

    pl.semaphore_wait(barrier, depth + 1)

    sib = []
    for rel in range(COLS):
        which = col if rel == 0 else 1 - col
        sib.append(send(pair_ref.at[:, :, which, 1 - core], pair_sib.at[:, rel],
                        sib_send.at[rel], sib_recv.at[rel], sibling))
    sib.append(send(left_ref, left_sib, sib_send.at[2], sib_recv.at[2], sibling))
    gather_z = [
        send(gathered.at[:, 0, z], gathered.at[:, 0, z], agz_send.at[d - 1], agz_recv.at[d - 1],
             at_z(z_peer(d)))
        for d in range(1, depth)
    ]
    gather_y = []
    for d in range(depth):
        other = z if d == 0 else lax.rem(z + depth - d, depth)
        gather_y.append(send(gathered.at[:, 0, other], gathered.at[:, 1, other],
                             agy_send.at[d], agy_recv.at[d], across))
    for copy in gather_z:
        copy.start()
    for copy in sib:
        copy.start()
    gather_y[0].start()

    weight_f32[...] = weight_ref[...].astype(F32)
    for e in range(C):
        weight_perm[e * C:(e + 1) * C, :] = weight_f32[pl.ds(e, C, stride=C), :].astype(BF16)

    rows_g = C // GROUPS * C

    def project(g, pair, first):
        taps = weight_perm[g * rows_g:(g + 1) * rows_g, :]

        def step(t, carry):
            slab = pair[pl.ds(2 * t, 2)].reshape(2 * width, -1)
            res = lax.dot_general(taps, slab, (((1,), (1,)), ((), ())),
                                  preferred_element_type=F32).astype(BF16)
            for k in range(2):
                row = pl.multiple_of(first + (2 * t + k) * C, C)
                for q in range(C // GROUPS):
                    e = g * (C // GROUPS) + q
                    grad[pl.ds(row, C), e * width:(e + 1) * width] = (
                        res[q * C:(q + 1) * C, k * width:(k + 1) * width])
            return carry

        lax.fori_loop(0, block // 2, step, 0, unroll=2)

    reduce_y = [send(y_send.at[g], y_recv.at[g], rsy_send.at[g], rsy_recv.at[g], across)
                for g in range(GROUPS)]
    reduce_z = [
        [send(z_send.at[g, z_peer(d)], z_recv.at[g, d - 1],
              rsz_send.at[g, d - 1], rsz_recv.at[g, d - 1], at_z(z_peer(d)))
         for d in range(1, depth)]
        for g in range(GROUPS)
    ]

    def columns(g):
        part = slice(g * per_group * 2 * width, (g + 1) * per_group * 2 * width)
        res = jnp.dot(left_ref[...], grad[:chans, part], preferred_element_type=F32)
        res += jnp.dot(left_sib[...], grad[chans:, part], preferred_element_type=F32)
        for q in range(per_group):
            at = 2 * q * width
            turned = jnp.concatenate(
                [res[:, at:at + width], res[:, at + width:at + 2 * width]], axis=0).T
            where = slice(q * lanes, (q + 1) * lanes)
            column_sum[g, :, where] = turned[:span]
            y_send[g, :, where] = turned[span:].astype(BF16)
        reduce_y[g].start()

    def second(g):
        reduce_y[g].wait_recv()
        column_sum[g] += y_recv[g].astype(F32)
        for k in range(depth):
            z_send[g, k] = column_sum[g, k * block:(k + 1) * block, :].astype(BF16)
        for copy in reduce_z[g]:
            copy.start()

    def rows(first):
        part = per_group * 2 * width
        acc = None
        for g in range(GROUPS):
            term = jnp.dot(grad[first:first + chans, g * part:(g + 1) * part],
                           right_all[g * part:(g + 1) * part, :], preferred_element_type=F32)
            acc = term if acc is None else acc + term
        turned = acc.T
        return turned[:n_seq] + turned[n_seq:]

    for copy in loads:
        copy.wait()
    for g in range(GROUPS):
        project(g, pair_own, 0)
        if g == 0:
            for copy in sib:
                copy.wait_recv()
        project(g, pair_sib, chans)
        for d in range(1, depth):
            if (d - 1) * (GROUPS - 1) // (depth - 1) == g - 1:
                gather_z[d - 1].wait_recv()
                gather_y[d].start()
        columns(g)

    for copy in gather_y:
        copy.wait_recv()
    upper = lax.broadcasted_iota(jnp.int32, (width, lanes), 1) >= n_seq
    mask_odd = upper.astype(F32).astype(BF16)
    mask_even = (1.0 - upper.astype(F32)).astype(BF16)
    for ep in range(HALF):
        piece = gathered[ep].reshape(width, lanes)
        right_all[2 * ep * width:(2 * ep + 1) * width, :] = piece * mask_even
        right_all[(2 * ep + 1) * width:(2 * ep + 2) * width, :] = piece * mask_odd

    for g in range(GROUPS - 1):
        second(g)
    left_send[...] = rows(chans)
    exchange = send(left_send, left_recv, sib_send.at[3], sib_recv.at[3], sibling)
    exchange.start()
    second(GROUPS - 1)
    mine = rows(0)
    exchange.wait_recv()
    out[0] = ((mine + left_recv[...]) * (1.0 / n_seq)).astype(BF16)

    for g in range(GROUPS):
        acc = column_sum[g, pl.ds(pl.multiple_of(z * block, block), block), :]
        for d in range(1, depth):
            reduce_z[g][d - 1].wait_recv()
            acc += z_recv[g, d - 1].astype(F32)
        for q in range(per_group):
            ep = g * per_group + q
            tile = acc[:, q * lanes:(q + 1) * lanes] * (1.0 / n_seq)
            rows_f32[pl.ds(2 * ep, block, stride=C), :] = tile
            rows_f32[pl.ds(2 * ep + 1, block, stride=C), :] = pltpu.roll(tile, n_seq, 1)
    out[1] = rows_f32[...].T[:n_seq].astype(BF16)

    for copy in sib + gather_z + gather_y + reduce_y + [exchange]:
        copy.wait_send()
    for group in reduce_z:
        for copy in group:
            copy.wait_send()


def per_device(n_row, left_proj, right_proj, pair_cot, out_weight):
    n_seq = left_proj.shape[0]
    block, total, p_size = pair_cot.shape
    depth = n_row // (CORES * COLS)
    span = depth * block
    width = COLS * span
    chans = block * C
    lanes = 2 * n_seq
    group_lanes = HALF // GROUPS * lanes
    pair = pair_cot.reshape(block, depth, COLS, CORES, block, p_size)
    vmem = pl.BlockSpec(memory_space=pltpu.VMEM)
    dma = pltpu.SemaphoreType.DMA
    flops = 2 * block * total * C * C * (p_size + 2 * n_seq)
    scratch = [
        pltpu.VMEM((block, COLS, depth, block, p_size), BF16),
        pltpu.VMEM((block, COLS, depth, block, p_size), BF16),
        pltpu.VMEM((n_seq, chans), BF16),
        pltpu.VMEM((C * C, p_size), F32),
        pltpu.VMEM((C * C, p_size), BF16),
        pltpu.VMEM((2 * chans, C * width), BF16),
        pltpu.VMEM((chans, lanes), F32),
        pltpu.VMEM((HALF, COLS, depth, block, lanes), BF16),
        pltpu.VMEM((C * width, lanes), BF16),
        pltpu.VMEM((GROUPS, span, group_lanes), F32),
        pltpu.VMEM((GROUPS, span, group_lanes), BF16),
        pltpu.VMEM((GROUPS, span, group_lanes), BF16),
        pltpu.VMEM((GROUPS, depth, block, group_lanes), BF16),
        pltpu.VMEM((GROUPS, depth - 1, block, group_lanes), BF16),
        pltpu.VMEM((n_seq, chans), F32),
        pltpu.VMEM((n_seq, chans), F32),
        dma((COLS,)),
        dma((4,)), dma((4,)),
        dma((depth - 1,)), dma((depth - 1,)),
        dma((depth,)), dma((depth,)),
        dma((GROUPS,)), dma((GROUPS,)),
        dma((GROUPS, depth - 1)), dma((GROUPS, depth - 1)),
    ]
    held = sum(2 * math.prod(b.shape) if b.dtype == BF16 else 4 * math.prod(b.shape)
               for b in scratch if b.dtype in (BF16, F32))
    held += 2 * 2 * (left_proj.size * 4 + out_weight.size)
    sums = pl.pallas_call(
        functools.partial(kernel, depth, n_seq, block),
        out_shape=jax.ShapeDtypeStruct((2, n_seq, chans), BF16),
        in_specs=[vmem, vmem, pl.BlockSpec(memory_space=pltpu.HBM), vmem],
        out_specs=vmem,
        scratch_shapes=scratch,
        compiler_params=pltpu.CompilerParams(
            collective_id=0, has_side_effects=True, vmem_limit_bytes=held + 4 * 1024 * 1024
        ),
        cost_estimate=pl.CostEstimate(
            flops=flops, bytes_accessed=4 * pair_cot.size, transcendentals=0
        ),
    )(left_proj, right_proj, pair, out_weight)
    return (sums[0], sums[1])


def solution(mesh):
    return jax.shard_map(
        functools.partial(per_device, mesh.shape["row"]),
        mesh=mesh,
        in_specs=(P("groups", "row"), P("groups", "row"), P(("groups", "row"), None, None), P()),
        out_specs=(P("groups", "row"), P("groups", "row")),
        check_vma=False,
    )
```

```python
import functools
import math

import jax
import jax.numpy as jnp
from jax import lax
from jax.experimental import pallas as pl
from jax.experimental.pallas import tpu as pltpu
from jax.sharding import PartitionSpec as P

C = 32
CORES = 2
COLS = 2
HALF = C // 2
GROUPS = 4
MESH = pl.DeviceIdType.MESH
F32 = jnp.float32
BF16 = jnp.bfloat16


def kernel(
    depth, n_seq, block,
    left_hbm, right_hbm, pair_ref, weight_hbm,
    out,
    left_ref, right_ref, weight_ref,
    pair_own, pair_sib, left_sib, weight_f32, weight_perm, grad, rows_f32,
    gathered, right_all, column_sum, y_send, y_recv, z_send, z_recv,
    left_send, left_recv,
    load_sem, sib_send, sib_recv, agz_send, agz_recv, agy_send, agy_recv,
    rsy_send, rsy_recv, rsz_send, rsz_recv,
):
    me = lax.axis_index("row")
    core = lax.rem(me, CORES)
    col = lax.rem(me // CORES, COLS)
    z = me // (CORES * COLS)
    sibling = me + 1 - 2 * core
    across = me + CORES * (1 - 2 * col)
    span = depth * block
    width = COLS * span
    chans = block * C
    lanes = 2 * n_seq
    per_group = HALF // GROUPS
    group_lanes = per_group * lanes

    def z_peer(step):
        return lax.rem(z + step, depth)

    def at_z(other):
        return other * (CORES * COLS) + lax.rem(me, CORES * COLS)

    def send(src, dst, s_sem, r_sem, target):
        return pltpu.make_async_remote_copy(
            src_ref=src, dst_ref=dst, send_sem=s_sem, recv_sem=r_sem,
            device_id={"row": target}, device_id_type=MESH,
        )

    barrier = pltpu.get_barrier_semaphore()
    for target in [sibling, across] + [at_z(z_peer(d)) for d in range(1, depth)]:
        pl.semaphore_signal(barrier, inc=1, device_id={"row": target}, device_id_type=MESH)

    load_right = pltpu.make_async_copy(right_hbm, right_ref, load_sem.at[COLS])
    load_weight = pltpu.make_async_copy(weight_hbm, weight_ref, load_sem.at[COLS + 1])
    load_left = pltpu.make_async_copy(left_hbm, left_ref, load_sem.at[COLS + 2])
    loads = [load_left]
    for rel in range(COLS):
        which = col if rel == 0 else 1 - col
        loads.append(pltpu.make_async_copy(
            pair_ref.at[:, :, which, core], pair_own.at[:, rel], load_sem.at[rel]))
    for copy in [load_right, load_weight] + loads:
        copy.start()

    pl.semaphore_wait(barrier, depth + 1)

    sib = []
    for rel in range(COLS):
        which = col if rel == 0 else 1 - col
        sib.append(send(pair_ref.at[:, :, which, 1 - core], pair_sib.at[:, rel],
                        sib_send.at[rel], sib_recv.at[rel], sibling))
    sib.append(send(left_hbm, left_sib, sib_send.at[2], sib_recv.at[2], sibling))
    for copy in sib:
        copy.start()

    load_right.wait()
    wide = right_ref[...].astype(F32)
    rows_f32[...] = jnp.concatenate([wide, wide], axis=0).T
    low = lax.broadcasted_iota(jnp.int32, (block, lanes), 1) < n_seq
    for ep in range(HALF):
        even = rows_f32[pl.ds(2 * ep, block, stride=C), :]
        odd = rows_f32[pl.ds(2 * ep + 1, block, stride=C), :]
        gathered[ep, 0, z] = jnp.where(low, even, odd).astype(BF16)

    gather_z = [
        send(gathered.at[:, 0, z], gathered.at[:, 0, z], agz_send.at[d - 1], agz_recv.at[d - 1],
             at_z(z_peer(d)))
        for d in range(1, depth)
    ]
    gather_y = []
    for d in range(depth):
        other = z if d == 0 else lax.rem(z + depth - d, depth)
        gather_y.append(send(gathered.at[:, 0, other], gathered.at[:, 1, other],
                             agy_send.at[d], agy_recv.at[d], across))
    for copy in gather_z:
        copy.start()
    gather_y[0].start()

    load_weight.wait()
    weight_f32[...] = weight_ref[...].astype(F32)
    for e in range(C):
        weight_perm[e * C:(e + 1) * C, :] = weight_f32[pl.ds(e, C, stride=C), :].astype(BF16)

    rows_g = C // GROUPS * C

    def project(g, pair, first):
        taps = weight_perm[g * rows_g:(g + 1) * rows_g, :]

        def step(t, carry):
            slab = pair[pl.ds(2 * t, 2)].reshape(2 * width, -1)
            res = lax.dot_general(taps, slab, (((1,), (1,)), ((), ())),
                                  preferred_element_type=F32).astype(BF16)
            for k in range(2):
                row = pl.multiple_of(first + (2 * t + k) * C, C)
                for q in range(C // GROUPS):
                    e = g * (C // GROUPS) + q
                    grad[pl.ds(row, C), e * width:(e + 1) * width] = (
                        res[q * C:(q + 1) * C, k * width:(k + 1) * width])
            return carry

        lax.fori_loop(0, block // 2, step, 0, unroll=4)

    reduce_y = [send(y_send.at[g], y_recv.at[g], rsy_send.at[g], rsy_recv.at[g], across)
                for g in range(GROUPS)]
    reduce_z = [
        [send(z_send.at[g, z_peer(d)], z_recv.at[g, d - 1],
              rsz_send.at[g, d - 1], rsz_recv.at[g, d - 1], at_z(z_peer(d)))
         for d in range(1, depth)]
        for g in range(GROUPS)
    ]

    def columns(g):
        part = slice(g * per_group * 2 * width, (g + 1) * per_group * 2 * width)
        res = jnp.dot(left_ref[...], grad[:chans, part], preferred_element_type=F32)
        res += jnp.dot(left_sib[...], grad[chans:, part], preferred_element_type=F32)
        for q in range(per_group):
            at = 2 * q * width
            turned = jnp.concatenate(
                [res[:, at:at + width], res[:, at + width:at + 2 * width]], axis=0).T
            where = slice(q * lanes, (q + 1) * lanes)
            column_sum[g, :, where] = turned[:span]
            y_send[g, :, where] = turned[span:].astype(BF16)
        reduce_y[g].start()

    def second(g):
        reduce_y[g].wait_recv()
        column_sum[g] += y_recv[g].astype(F32)
        for k in range(depth):
            z_send[g, k] = column_sum[g, k * block:(k + 1) * block, :].astype(BF16)
        for copy in reduce_z[g]:
            copy.start()

    def rows(first):
        part = per_group * 2 * width
        acc = None
        for g in range(GROUPS):
            term = jnp.dot(grad[first:first + chans, g * part:(g + 1) * part],
                           right_all[g * part:(g + 1) * part, :], preferred_element_type=F32)
            acc = term if acc is None else acc + term
        turned = acc.T
        return turned[:n_seq] + turned[n_seq:]

    for copy in loads:
        copy.wait()
    for g in range(GROUPS // 2):
        project(g, pair_own, 0)
    for copy in sib:
        copy.wait_recv()
    for g in range(GROUPS):
        if g >= GROUPS // 2:
            project(g, pair_own, 0)
        project(g, pair_sib, chans)
        for d in range(1, depth):
            if (d - 1) * (GROUPS - 1) // (depth - 1) == g - 1:
                gather_z[d - 1].wait_recv()
                gather_y[d].start()
        columns(g)
        if g >= 2:
            second(g - 2)

    for copy in gather_y:
        copy.wait_recv()
    upper = lax.broadcasted_iota(jnp.int32, (width, lanes), 1) >= n_seq
    mask_odd = upper.astype(F32).astype(BF16)
    mask_even = (1.0 - upper.astype(F32)).astype(BF16)
    for ep in range(HALF):
        piece = gathered[ep].reshape(width, lanes)
        right_all[2 * ep * width:(2 * ep + 1) * width, :] = piece * mask_even
        right_all[(2 * ep + 1) * width:(2 * ep + 2) * width, :] = piece * mask_odd

    left_send[...] = rows(chans)
    exchange = send(left_send, left_recv, sib_send.at[3], sib_recv.at[3], sibling)
    exchange.start()
    second(GROUPS - 2)
    second(GROUPS - 1)
    mine = rows(0)
    exchange.wait_recv()
    out[0] = ((mine + left_recv[...]) * (1.0 / n_seq)).astype(BF16)

    for g in range(GROUPS):
        acc = column_sum[g, pl.ds(pl.multiple_of(z * block, block), block), :]
        for d in range(1, depth):
            reduce_z[g][d - 1].wait_recv()
            acc += z_recv[g, d - 1].astype(F32)
        for q in range(per_group):
            ep = g * per_group + q
            tile = acc[:, q * lanes:(q + 1) * lanes] * (1.0 / n_seq)
            rows_f32[pl.ds(2 * ep, block, stride=C), :] = tile
            rows_f32[pl.ds(2 * ep + 1, block, stride=C), :] = pltpu.roll(tile, n_seq, 1)
    out[1] = rows_f32[...].T[:n_seq].astype(BF16)

    for copy in sib + gather_z + gather_y + reduce_y + [exchange]:
        copy.wait_send()
    for group in reduce_z:
        for copy in group:
            copy.wait_send()


def per_device(n_row, left_proj, right_proj, pair_cot, out_weight):
    n_seq = left_proj.shape[0]
    block, total, p_size = pair_cot.shape
    depth = n_row // (CORES * COLS)
    span = depth * block
    width = COLS * span
    chans = block * C
    lanes = 2 * n_seq
    group_lanes = HALF // GROUPS * lanes
    pair = pair_cot.reshape(block, depth, COLS, CORES, block, p_size)
    vmem = pl.BlockSpec(memory_space=pltpu.VMEM)
    dma = pltpu.SemaphoreType.DMA
    flops = 2 * block * total * C * C * (p_size + 2 * n_seq)
    scratch = [
        pltpu.VMEM(left_proj.shape, BF16),
        pltpu.VMEM(right_proj.shape, BF16),
        pltpu.VMEM(out_weight.shape, BF16),
        pltpu.VMEM((block, COLS, depth, block, p_size), BF16),
        pltpu.VMEM((block, COLS, depth, block, p_size), BF16),
        pltpu.VMEM((n_seq, chans), BF16),
        pltpu.VMEM((C * C, p_size), F32),
        pltpu.VMEM((C * C, p_size), BF16),
        pltpu.VMEM((2 * chans, C * width), BF16),
        pltpu.VMEM((chans, lanes), F32),
        pltpu.VMEM((HALF, COLS, depth, block, lanes), BF16),
        pltpu.VMEM((C * width, lanes), BF16),
        pltpu.VMEM((GROUPS, span, group_lanes), F32),
        pltpu.VMEM((GROUPS, span, group_lanes), BF16),
        pltpu.VMEM((GROUPS, span, group_lanes), BF16),
        pltpu.VMEM((GROUPS, depth, block, group_lanes), BF16),
        pltpu.VMEM((GROUPS, depth - 1, block, group_lanes), BF16),
        pltpu.VMEM((n_seq, chans), F32),
        pltpu.VMEM((n_seq, chans), F32),
        dma((COLS + 3,)),
        dma((4,)), dma((4,)),
        dma((depth - 1,)), dma((depth - 1,)),
        dma((depth,)), dma((depth,)),
        dma((GROUPS,)), dma((GROUPS,)),
        dma((GROUPS, depth - 1)), dma((GROUPS, depth - 1)),
    ]
    held = sum(2 * math.prod(b.shape) if b.dtype == BF16 else 4 * math.prod(b.shape)
               for b in scratch if b.dtype in (BF16, F32))
    held += 8 * left_proj.size
    sums = pl.pallas_call(
        functools.partial(kernel, depth, n_seq, block),
        out_shape=pltpu.VMEM((2, n_seq, chans), BF16),
        in_specs=[pl.BlockSpec(memory_space=pltpu.HBM)] * 4,
        out_specs=vmem,
        scratch_shapes=scratch,
        compiler_params=pltpu.CompilerParams(
            collective_id=0, has_side_effects=True, vmem_limit_bytes=held + 4 * 1024 * 1024
        ),
        cost_estimate=pl.CostEstimate(
            flops=flops, bytes_accessed=4 * pair_cot.size, transcendentals=0
        ),
    )(*[pltpu.with_memory_space_constraint(x, pltpu.HBM)
        for x in (left_proj, right_proj, pair, out_weight)])
    return (sums[0], sums[1])


def solution(mesh):
    return jax.shard_map(
        functools.partial(per_device, mesh.shape["row"]),
        mesh=mesh,
        in_specs=(P("groups", "row"), P("groups", "row"), P(("groups", "row"), None, None), P()),
        out_specs=(P("groups", "row"), P("groups", "row")),
        check_vma=False,
    )
```

```python
import functools
import math

import jax
import jax.numpy as jnp
from jax import lax
from jax.experimental import pallas as pl
from jax.experimental.pallas import tpu as pltpu
from jax.sharding import PartitionSpec as P

C = 32
CORES = 2
COLS = 2
HALF = C // 2
GROUPS = 4
MESH = pl.DeviceIdType.MESH
F32 = jnp.float32
BF16 = jnp.bfloat16


def kernel(
    depth, n_seq, block,
    left_hbm, right_hbm, pair_ref, weight_hbm,
    out,
    left_ref, right_ref, weight_ref,
    pair_own, pair_sib, left_sib, weight_f32, weight_perm, grad_a, grad_b, grad_c, grad_d, rows_f32,
    gathered, right_all, column_sum, y_send, y_recv, z_send, z_recv,
    left_send, left_recv,
    load_sem, sib_send, sib_recv, agz_send, agz_recv, agy_send, agy_recv,
    rsy_send, rsy_recv, rsz_send, rsz_recv,
):
    me = lax.axis_index("row")
    core = lax.rem(me, CORES)
    col = lax.rem(me // CORES, COLS)
    z = me // (CORES * COLS)
    sibling = me + 1 - 2 * core
    across = me + CORES * (1 - 2 * col)
    span = depth * block
    width = COLS * span
    chans = block * C
    lanes = 2 * n_seq
    per_group = HALF // GROUPS
    group_lanes = per_group * lanes

    def z_peer(step):
        return lax.rem(z + step, depth)

    def at_z(other):
        return other * (CORES * COLS) + lax.rem(me, CORES * COLS)

    def send(src, dst, s_sem, r_sem, target):
        return pltpu.make_async_remote_copy(
            src_ref=src, dst_ref=dst, send_sem=s_sem, recv_sem=r_sem,
            device_id={"row": target}, device_id_type=MESH,
        )

    barrier = pltpu.get_barrier_semaphore()
    for target in [sibling, across] + [at_z(z_peer(d)) for d in range(1, depth)]:
        pl.semaphore_signal(barrier, inc=1, device_id={"row": target}, device_id_type=MESH)

    load_right = pltpu.make_async_copy(right_hbm, right_ref, load_sem.at[COLS])
    load_weight = pltpu.make_async_copy(weight_hbm, weight_ref, load_sem.at[COLS + 1])
    load_left = pltpu.make_async_copy(left_hbm, left_ref, load_sem.at[COLS + 2])
    loads = [load_left]
    for rel in range(COLS):
        which = col if rel == 0 else 1 - col
        loads.append(pltpu.make_async_copy(
            pair_ref.at[:, :, which, core], pair_own.at[:, rel], load_sem.at[rel]))
    for copy in [load_right, load_weight] + loads:
        copy.start()

    pl.semaphore_wait(barrier, depth + 1)

    sib = []
    for rel in range(COLS):
        which = col if rel == 0 else 1 - col
        sib.append(send(pair_ref.at[:, :, which, 1 - core], pair_sib.at[:, rel],
                        sib_send.at[rel], sib_recv.at[rel], sibling))
    sib.append(send(left_hbm, left_sib, sib_send.at[2], sib_recv.at[2], sibling))
    for copy in sib:
        copy.start()

    load_right.wait()
    wide = right_ref[...].astype(F32)
    rows_f32[...] = jnp.concatenate([wide, wide], axis=0).T
    low = lax.broadcasted_iota(jnp.int32, (block, lanes), 1) < n_seq
    for ep in range(HALF):
        even = rows_f32[pl.ds(2 * ep, block, stride=C), :]
        odd = rows_f32[pl.ds(2 * ep + 1, block, stride=C), :]
        gathered[ep, 0, z] = jnp.where(low, even, odd).astype(BF16)

    gather_z = [
        send(gathered.at[:, 0, z], gathered.at[:, 0, z], agz_send.at[d - 1], agz_recv.at[d - 1],
             at_z(z_peer(d)))
        for d in range(1, depth)
    ]
    gather_y = []
    for d in range(depth):
        other = z if d == 0 else lax.rem(z + depth - d, depth)
        gather_y.append(send(gathered.at[:, 0, other], gathered.at[:, 1, other],
                             agy_send.at[d], agy_recv.at[d], across))
    for copy in gather_z:
        copy.start()
    gather_y[0].start()

    load_weight.wait()
    weight_f32[...] = weight_ref[...].astype(F32)
    for e in range(C):
        weight_perm[e * C:(e + 1) * C, :] = weight_f32[pl.ds(e, C, stride=C), :].astype(BF16)

    rows_g = C // GROUPS * C
    grads = (grad_a, grad_b, grad_c, grad_d)

    def project(g, pair, first):
        taps = weight_perm[g * rows_g:(g + 1) * rows_g, :]

        def step(t, carry):
            slab = pair[pl.ds(2 * t, 2)].reshape(2 * width, -1)
            res = lax.dot_general(taps, slab, (((1,), (1,)), ((), ())),
                                  preferred_element_type=F32).astype(BF16)
            for k in range(2):
                row = first + (2 * t + k) * C
                if not isinstance(t, int):
                    row = pl.multiple_of(row, C)
                for q in range(C // GROUPS):
                    grads[g][pl.ds(row, C), q * width:(q + 1) * width] = (
                        res[q * C:(q + 1) * C, k * width:(k + 1) * width])
            return carry

        if width <= 128:
            for t in range(block // 2):
                step(t, 0)
        else:
            lax.fori_loop(0, block // 2, step, 0, unroll=2)

    reduce_y = [send(y_send.at[g], y_recv.at[g], rsy_send.at[g], rsy_recv.at[g], across)
                for g in range(GROUPS)]
    reduce_z = [
        [send(z_send.at[g, z_peer(d)], z_recv.at[g, d - 1],
              rsz_send.at[g, d - 1], rsz_recv.at[g, d - 1], at_z(z_peer(d)))
         for d in range(1, depth)]
        for g in range(GROUPS)
    ]

    def columns(g):
        res = jnp.dot(left_ref[...], grads[g][:chans, :], preferred_element_type=F32)
        res += jnp.dot(left_sib[...], grads[g][chans:, :], preferred_element_type=F32)
        for q in range(per_group):
            at = 2 * q * width
            turned = jnp.concatenate(
                [res[:, at:at + width], res[:, at + width:at + 2 * width]], axis=0).T
            where = slice(q * lanes, (q + 1) * lanes)
            column_sum[g, :, where] = turned[:span]
            y_send[g, :, where] = turned[span:].astype(BF16)

    def second(g):
        reduce_y[g].wait_recv()
        column_sum[g] += y_recv[g].astype(F32)
        for k in range(depth):
            z_send[g, k] = column_sum[g, k * block:(k + 1) * block, :].astype(BF16)
        for copy in reduce_z[g]:
            copy.start()

    def rows(first):
        part = per_group * 2 * width
        acc = None
        for g in range(GROUPS):
            term = jnp.dot(grads[g][first:first + chans, :],
                           right_all[g * part:(g + 1) * part, :], preferred_element_type=F32)
            acc = term if acc is None else acc + term
        turned = acc.T
        return turned[:n_seq] + turned[n_seq:]

    for copy in loads:
        copy.wait()
    for g in range(GROUPS // 2):
        project(g, pair_own, 0)
    for copy in sib:
        copy.wait_recv()
    project(0, pair_sib, chans)
    for g in range(GROUPS):
        if g + 1 < GROUPS:
            if g + 1 >= GROUPS // 2:
                project(g + 1, pair_own, 0)
            project(g + 1, pair_sib, chans)
        columns(g)
        reduce_y[g].start()
        for d in range(1, depth):
            if (d - 1) * (GROUPS - 1) // (depth - 1) == g:
                gather_z[d - 1].wait_recv()
                gather_y[d].start()
        if g >= 2:
            second(g - 2)

    for copy in gather_y:
        copy.wait_recv()
    upper = lax.broadcasted_iota(jnp.int32, (width, lanes), 1) >= n_seq
    mask_odd = upper.astype(F32).astype(BF16)
    mask_even = (1.0 - upper.astype(F32)).astype(BF16)
    for ep in range(HALF):
        piece = gathered[ep].reshape(width, lanes)
        right_all[2 * ep * width:(2 * ep + 1) * width, :] = piece * mask_even
        right_all[(2 * ep + 1) * width:(2 * ep + 2) * width, :] = piece * mask_odd

    left_send[...] = rows(chans)
    exchange = send(left_send, left_recv, sib_send.at[3], sib_recv.at[3], sibling)
    exchange.start()
    second(GROUPS - 2)
    second(GROUPS - 1)
    mine = rows(0)
    exchange.wait_recv()
    out[0] = ((mine + left_recv[...]) * (1.0 / n_seq)).astype(BF16)

    for g in range(GROUPS):
        acc = column_sum[g, pl.ds(pl.multiple_of(z * block, block), block), :]
        for d in range(1, depth):
            reduce_z[g][d - 1].wait_recv()
            acc += z_recv[g, d - 1].astype(F32)
        for q in range(per_group):
            ep = g * per_group + q
            tile = acc[:, q * lanes:(q + 1) * lanes] * (1.0 / n_seq)
            rows_f32[pl.ds(2 * ep, block, stride=C), :] = tile
            rows_f32[pl.ds(2 * ep + 1, block, stride=C), :] = pltpu.roll(tile, n_seq, 1)
    out[1] = rows_f32[...].T[:n_seq].astype(BF16)

    for copy in sib + gather_z + gather_y + reduce_y + [exchange]:
        copy.wait_send()
    for group in reduce_z:
        for copy in group:
            copy.wait_send()


def per_device(n_row, left_proj, right_proj, pair_cot, out_weight):
    n_seq = left_proj.shape[0]
    block, total, p_size = pair_cot.shape
    depth = n_row // (CORES * COLS)
    span = depth * block
    width = COLS * span
    chans = block * C
    lanes = 2 * n_seq
    group_lanes = HALF // GROUPS * lanes
    pair = pair_cot.reshape(block, depth, COLS, CORES, block, p_size)
    vmem = pl.BlockSpec(memory_space=pltpu.VMEM)
    dma = pltpu.SemaphoreType.DMA
    flops = 2 * block * total * C * C * (p_size + 2 * n_seq)
    scratch = [
        pltpu.VMEM(left_proj.shape, BF16),
        pltpu.VMEM(right_proj.shape, BF16),
        pltpu.VMEM(out_weight.shape, BF16),
        pltpu.VMEM((block, COLS, depth, block, p_size), BF16),
        pltpu.VMEM((block, COLS, depth, block, p_size), BF16),
        pltpu.VMEM((n_seq, chans), BF16),
        pltpu.VMEM((C * C, p_size), F32),
        pltpu.VMEM((C * C, p_size), BF16),
        *[pltpu.VMEM((2 * chans, C // GROUPS * width), BF16)] * GROUPS,
        pltpu.VMEM((chans, lanes), F32),
        pltpu.VMEM((HALF, COLS, depth, block, lanes), BF16),
        pltpu.VMEM((C * width, lanes), BF16),
        pltpu.VMEM((GROUPS, span, group_lanes), F32),
        pltpu.VMEM((GROUPS, span, group_lanes), BF16),
        pltpu.VMEM((GROUPS, span, group_lanes), BF16),
        pltpu.VMEM((GROUPS, depth, block, group_lanes), BF16),
        pltpu.VMEM((GROUPS, depth - 1, block, group_lanes), BF16),
        pltpu.VMEM((n_seq, chans), F32),
        pltpu.VMEM((n_seq, chans), F32),
        dma((COLS + 3,)),
        dma((4,)), dma((4,)),
        dma((depth - 1,)), dma((depth - 1,)),
        dma((depth,)), dma((depth,)),
        dma((GROUPS,)), dma((GROUPS,)),
        dma((GROUPS, depth - 1)), dma((GROUPS, depth - 1)),
    ]
    held = sum(2 * math.prod(b.shape) if b.dtype == BF16 else 4 * math.prod(b.shape)
               for b in scratch if b.dtype in (BF16, F32))
    held += 8 * left_proj.size
    sums = pl.pallas_call(
        functools.partial(kernel, depth, n_seq, block),
        out_shape=pltpu.VMEM((2, n_seq, chans), BF16),
        in_specs=[pl.BlockSpec(memory_space=pltpu.HBM)] * 4,
        out_specs=vmem,
        scratch_shapes=scratch,
        compiler_params=pltpu.CompilerParams(
            collective_id=0, has_side_effects=True, vmem_limit_bytes=held + 4 * 1024 * 1024
        ),
        cost_estimate=pl.CostEstimate(
            flops=flops, bytes_accessed=4 * pair_cot.size, transcendentals=0
        ),
    )(*[pltpu.with_memory_space_constraint(x, pltpu.HBM)
        for x in (left_proj, right_proj, pair, out_weight)])
    return (sums[0], sums[1])


def solution(mesh):
    return jax.shard_map(
        functools.partial(per_device, mesh.shape["row"]),
        mesh=mesh,
        in_specs=(P("groups", "row"), P("groups", "row"), P(("groups", "row"), None, None), P()),
        out_specs=(P("groups", "row"), P("groups", "row")),
        check_vma=False,
    )
```

```python
import functools
import math

import jax
import jax.numpy as jnp
from jax import lax
from jax.experimental import pallas as pl
from jax.experimental.pallas import tpu as pltpu
from jax.sharding import PartitionSpec as P

C = 32
CORES = 2
COLS = 2
HALF = C // 2
GROUPS = 4
MESH = pl.DeviceIdType.MESH
F32 = jnp.float32
BF16 = jnp.bfloat16


def kernel(
    depth, n_seq, block,
    left_hbm, right_hbm, pair_ref, weight_hbm,
    out,
    left_ref, right_ref, weight_ref,
    pair_own, pair_sib, left_sib, weight_f32, weight_perm, grad_a, grad_b, grad_c, grad_d, rows_f32,
    gathered, right_all, column_sum, y_send, y_recv, z_send, z_recv,
    left_send, left_recv,
    load_sem, sib_send, sib_recv, agz_send, agz_recv, agy_send, agy_recv,
    rsy_send, rsy_recv, rsz_send, rsz_recv,
):
    me = lax.axis_index("row")
    core = lax.rem(me, CORES)
    col = lax.rem(me // CORES, COLS)
    z = me // (CORES * COLS)
    sibling = me + 1 - 2 * core
    across = me + CORES * (1 - 2 * col)
    span = depth * block
    width = COLS * span
    chans = block * C
    lanes = 2 * n_seq
    per_group = HALF // GROUPS
    group_lanes = per_group * lanes

    def z_peer(step):
        return lax.rem(z + step, depth)

    def at_z(other):
        return other * (CORES * COLS) + lax.rem(me, CORES * COLS)

    def send(src, dst, s_sem, r_sem, target):
        return pltpu.make_async_remote_copy(
            src_ref=src, dst_ref=dst, send_sem=s_sem, recv_sem=r_sem,
            device_id={"row": target}, device_id_type=MESH,
        )

    barrier = pltpu.get_barrier_semaphore()
    for target in [sibling, across] + [at_z(z_peer(d)) for d in range(1, depth)]:
        pl.semaphore_signal(barrier, inc=1, device_id={"row": target}, device_id_type=MESH)

    load_right = pltpu.make_async_copy(right_hbm, right_ref, load_sem.at[COLS])
    load_weight = pltpu.make_async_copy(weight_hbm, weight_ref, load_sem.at[COLS + 1])
    load_left = pltpu.make_async_copy(left_hbm, left_ref, load_sem.at[COLS + 2])
    loads = [load_left]
    for rel in range(COLS):
        which = col if rel == 0 else 1 - col
        loads.append(pltpu.make_async_copy(
            pair_ref.at[:, :, which, core], pair_own.at[:, rel], load_sem.at[rel]))
    for copy in [load_right, load_weight] + loads:
        copy.start()

    pl.semaphore_wait(barrier, depth + 1)

    sib = []
    for rel in range(COLS):
        which = col if rel == 0 else 1 - col
        sib.append(send(pair_ref.at[:, :, which, 1 - core], pair_sib.at[:, rel],
                        sib_send.at[rel], sib_recv.at[rel], sibling))
    sib.append(send(left_hbm, left_sib, sib_send.at[2], sib_recv.at[2], sibling))
    for copy in sib:
        copy.start()

    load_right.wait()
    wide = right_ref[...].astype(F32)
    rows_f32[...] = jnp.concatenate([wide, wide], axis=0).T
    low = lax.broadcasted_iota(jnp.int32, (block, lanes), 1) < n_seq
    for ep in range(HALF):
        even = rows_f32[pl.ds(2 * ep, block, stride=C), :]
        odd = rows_f32[pl.ds(2 * ep + 1, block, stride=C), :]
        gathered[ep, 0, z] = jnp.where(low, even, odd).astype(BF16)

    def nearest(k):
        both = jnp.minimum(z, depth - 1 - z)
        toward = jnp.where(z < depth - 1 - z, 1, -1)
        near = z + (k + 1) // 2 * (1 if k % 2 else -1)
        return jnp.where(k <= 2 * both, near, z + toward * (k - both))

    gather_z = []
    gather_y = [send(gathered.at[:, 0, z], gathered.at[:, 1, z],
                     agy_send.at[z], agy_recv.at[z], across)]
    arrive_z = []
    for k in range(1, depth):
        other = nearest(k)
        gather_z.append(send(gathered.at[:, 0, z], gathered.at[:, 0, z],
                             agz_send.at[other], agz_recv.at[z], at_z(other)))
        arrive_z.append(send(gathered.at[:, 0, other], gathered.at[:, 0, other],
                             agz_send.at[other], agz_recv.at[other], at_z(other)))
        gather_y.append(send(gathered.at[:, 0, other], gathered.at[:, 1, other],
                             agy_send.at[other], agy_recv.at[other], across))
    for copy in gather_z:
        copy.start()
    gather_y[0].start()

    load_weight.wait()
    weight_f32[...] = weight_ref[...].astype(F32)
    for e in range(C):
        weight_perm[e * C:(e + 1) * C, :] = weight_f32[pl.ds(e, C, stride=C), :].astype(BF16)

    rows_g = C // GROUPS * C
    grads = (grad_a, grad_b, grad_c, grad_d)

    def project(g, pair, first):
        taps = weight_perm[g * rows_g:(g + 1) * rows_g, :]

        def step(t, carry):
            slab = pair[pl.ds(2 * t, 2)].reshape(2 * width, -1)
            res = lax.dot_general(taps, slab, (((1,), (1,)), ((), ())),
                                  preferred_element_type=F32).astype(BF16)
            for k in range(2):
                row = first + (2 * t + k) * C
                if not isinstance(t, int):
                    row = pl.multiple_of(row, C)
                for q in range(C // GROUPS):
                    grads[g][pl.ds(row, C), q * width:(q + 1) * width] = (
                        res[q * C:(q + 1) * C, k * width:(k + 1) * width])
            return carry

        if width <= 128:
            for t in range(block // 2):
                step(t, 0)
        else:
            lax.fori_loop(0, block // 2, step, 0, unroll=2)

    reduce_y = [send(y_send.at[g], y_recv.at[g], rsy_send.at[g], rsy_recv.at[g], across)
                for g in range(GROUPS)]
    reduce_z = [
        [send(z_send.at[g, z_peer(d)], z_recv.at[g, d - 1],
              rsz_send.at[g, d - 1], rsz_recv.at[g, d - 1], at_z(z_peer(d)))
         for d in range(1, depth)]
        for g in range(GROUPS)
    ]

    def columns(g):
        res = jnp.dot(left_ref[...], grads[g][:chans, :], preferred_element_type=F32)
        res += jnp.dot(left_sib[...], grads[g][chans:, :], preferred_element_type=F32)
        for q in range(per_group):
            at = 2 * q * width
            turned = jnp.concatenate(
                [res[:, at:at + width], res[:, at + width:at + 2 * width]], axis=0).T
            where = slice(q * lanes, (q + 1) * lanes)
            column_sum[g, :, where] = turned[:span]
            y_send[g, :, where] = turned[span:].astype(BF16)

    def second(g):
        reduce_y[g].wait_recv()
        column_sum[g] += y_recv[g].astype(F32)
        for k in range(depth):
            z_send[g, k] = column_sum[g, k * block:(k + 1) * block, :].astype(BF16)
        for copy in reduce_z[g]:
            copy.start()

    def rows(first):
        part = per_group * 2 * width
        acc = None
        for g in range(GROUPS):
            term = jnp.dot(grads[g][first:first + chans, :],
                           right_all[g * part:(g + 1) * part, :], preferred_element_type=F32)
            acc = term if acc is None else acc + term
        turned = acc.T
        return turned[:n_seq] + turned[n_seq:]

    for copy in loads:
        copy.wait()
    for g in range(GROUPS // 2):
        project(g, pair_own, 0)
    for copy in sib:
        copy.wait_recv()
    project(0, pair_sib, chans)
    for g in range(GROUPS):
        if g + 1 < GROUPS:
            if g + 1 >= GROUPS // 2:
                project(g + 1, pair_own, 0)
            project(g + 1, pair_sib, chans)
        columns(g)
        reduce_y[g].start()
        for d in range(1, depth):
            if max(1, (2 * d) // (depth - 1)) == g:
                arrive_z[d - 1].wait_recv()
                gather_y[d].start()
        if g >= 2:
            second(g - 2)

    for copy in gather_y:
        copy.wait_recv()
    upper = lax.broadcasted_iota(jnp.int32, (width, lanes), 1) >= n_seq
    mask_odd = upper.astype(F32).astype(BF16)
    mask_even = (1.0 - upper.astype(F32)).astype(BF16)
    for ep in range(HALF):
        piece = gathered[ep].reshape(width, lanes)
        right_all[2 * ep * width:(2 * ep + 1) * width, :] = piece * mask_even
        right_all[(2 * ep + 1) * width:(2 * ep + 2) * width, :] = piece * mask_odd

    left_send[...] = rows(chans)
    exchange = send(left_send, left_recv, sib_send.at[3], sib_recv.at[3], sibling)
    exchange.start()
    second(GROUPS - 2)
    second(GROUPS - 1)
    mine = rows(0)
    exchange.wait_recv()
    out[0] = ((mine + left_recv[...]) * (1.0 / n_seq)).astype(BF16)

    for g in range(GROUPS):
        acc = column_sum[g, pl.ds(pl.multiple_of(z * block, block), block), :]
        for d in range(1, depth):
            reduce_z[g][d - 1].wait_recv()
            acc += z_recv[g, d - 1].astype(F32)
        for q in range(per_group):
            ep = g * per_group + q
            tile = acc[:, q * lanes:(q + 1) * lanes] * (1.0 / n_seq)
            rows_f32[pl.ds(2 * ep, block, stride=C), :] = tile
            rows_f32[pl.ds(2 * ep + 1, block, stride=C), :] = pltpu.roll(tile, n_seq, 1)
    out[1] = rows_f32[...].T[:n_seq].astype(BF16)

    for copy in sib + gather_z + gather_y + reduce_y + [exchange]:
        copy.wait_send()
    for group in reduce_z:
        for copy in group:
            copy.wait_send()


def per_device(n_row, left_proj, right_proj, pair_cot, out_weight):
    n_seq = left_proj.shape[0]
    block, total, p_size = pair_cot.shape
    depth = n_row // (CORES * COLS)
    span = depth * block
    width = COLS * span
    chans = block * C
    lanes = 2 * n_seq
    group_lanes = HALF // GROUPS * lanes
    pair = pair_cot.reshape(block, depth, COLS, CORES, block, p_size)
    vmem = pl.BlockSpec(memory_space=pltpu.VMEM)
    dma = pltpu.SemaphoreType.DMA
    flops = 2 * block * total * C * C * (p_size + 2 * n_seq)
    scratch = [
        pltpu.VMEM(left_proj.shape, BF16),
        pltpu.VMEM(right_proj.shape, BF16),
        pltpu.VMEM(out_weight.shape, BF16),
        pltpu.VMEM((block, COLS, depth, block, p_size), BF16),
        pltpu.VMEM((block, COLS, depth, block, p_size), BF16),
        pltpu.VMEM((n_seq, chans), BF16),
        pltpu.VMEM((C * C, p_size), F32),
        pltpu.VMEM((C * C, p_size), BF16),
        *[pltpu.VMEM((2 * chans, C // GROUPS * width), BF16)] * GROUPS,
        pltpu.VMEM((chans, lanes), F32),
        pltpu.VMEM((HALF, COLS, depth, block, lanes), BF16),
        pltpu.VMEM((C * width, lanes), BF16),
        pltpu.VMEM((GROUPS, span, group_lanes), F32),
        pltpu.VMEM((GROUPS, span, group_lanes), BF16),
        pltpu.VMEM((GROUPS, span, group_lanes), BF16),
        pltpu.VMEM((GROUPS, depth, block, group_lanes), BF16),
        pltpu.VMEM((GROUPS, depth - 1, block, group_lanes), BF16),
        pltpu.VMEM((n_seq, chans), F32),
        pltpu.VMEM((n_seq, chans), F32),
        dma((COLS + 3,)),
        dma((4,)), dma((4,)),
        dma((depth,)), dma((depth,)),
        dma((depth,)), dma((depth,)),
        dma((GROUPS,)), dma((GROUPS,)),
        dma((GROUPS, depth - 1)), dma((GROUPS, depth - 1)),
    ]
    held = sum(2 * math.prod(b.shape) if b.dtype == BF16 else 4 * math.prod(b.shape)
               for b in scratch if b.dtype in (BF16, F32))
    held += 8 * left_proj.size
    sums = pl.pallas_call(
        functools.partial(kernel, depth, n_seq, block),
        out_shape=pltpu.VMEM((2, n_seq, chans), BF16),
        in_specs=[pl.BlockSpec(memory_space=pltpu.HBM)] * 4,
        out_specs=vmem,
        scratch_shapes=scratch,
        compiler_params=pltpu.CompilerParams(
            collective_id=0, has_side_effects=True, vmem_limit_bytes=held + 4 * 1024 * 1024
        ),
        cost_estimate=pl.CostEstimate(
            flops=flops, bytes_accessed=4 * pair_cot.size, transcendentals=0
        ),
    )(*[pltpu.with_memory_space_constraint(x, pltpu.HBM)
        for x in (left_proj, right_proj, pair, out_weight)])
    return (sums[0], sums[1])


def solution(mesh):
    return jax.shard_map(
        functools.partial(per_device, mesh.shape["row"]),
        mesh=mesh,
        in_specs=(P("groups", "row"), P("groups", "row"), P(("groups", "row"), None, None), P()),
        out_specs=(P("groups", "row"), P("groups", "row")),
        check_vma=False,
    )
```

```python
import functools
import math

import jax
import jax.numpy as jnp
from jax import lax
from jax.experimental import pallas as pl
from jax.experimental.pallas import tpu as pltpu
from jax.sharding import PartitionSpec as P

C = 32
CORES = 2
COLS = 2
HALF = C // 2
GROUPS = 4
MESH = pl.DeviceIdType.MESH
F32 = jnp.float32
BF16 = jnp.bfloat16


def kernel(
    depth, n_seq, block,
    left_hbm, right_hbm, pair_ref, weight_hbm,
    out,
    left_ref, right_ref, weight_ref,
    pair_own, pair_sib, left_sib, weight_f32, weight_perm, grad_a, grad_b, grad_c, grad_d, rows_f32,
    gathered, right_all, column_sum, y_send, y_recv, z_send, z_recv,
    left_send, left_recv,
    load_sem, sib_send, sib_recv, agz_send, agz_recv, agy_send, agy_recv,
    rsy_send, rsy_recv, rsz_send, rsz_recv,
):
    me = lax.axis_index("row")
    core = lax.rem(me, CORES)
    col = lax.rem(me // CORES, COLS)
    z = me // (CORES * COLS)
    sibling = me + 1 - 2 * core
    across = me + CORES * (1 - 2 * col)
    span = depth * block
    width = COLS * span
    chans = block * C
    lanes = 2 * n_seq
    per_group = HALF // GROUPS
    group_lanes = per_group * lanes

    def z_peer(step):
        return lax.rem(z + step, depth)

    def at_z(other):
        return other * (CORES * COLS) + lax.rem(me, CORES * COLS)

    def send(src, dst, s_sem, r_sem, target):
        return pltpu.make_async_remote_copy(
            src_ref=src, dst_ref=dst, send_sem=s_sem, recv_sem=r_sem,
            device_id={"row": target}, device_id_type=MESH,
        )

    barrier = pltpu.get_barrier_semaphore()
    for target in [sibling, across] + [at_z(z_peer(d)) for d in range(1, depth)]:
        pl.semaphore_signal(barrier, inc=1, device_id={"row": target}, device_id_type=MESH)

    load_right = pltpu.make_async_copy(right_hbm, right_ref, load_sem.at[COLS])
    load_weight = pltpu.make_async_copy(weight_hbm, weight_ref, load_sem.at[COLS + 1])
    load_left = pltpu.make_async_copy(left_hbm, left_ref, load_sem.at[COLS + 2])
    loads = [load_left]
    for rel in range(COLS):
        which = col if rel == 0 else 1 - col
        loads.append(pltpu.make_async_copy(
            pair_ref.at[:, :, which, core], pair_own.at[:, rel], load_sem.at[rel]))
    for copy in [load_right, load_weight] + loads:
        copy.start()

    pl.semaphore_wait(barrier, depth + 1)

    sib = []
    for rel in range(COLS):
        which = col if rel == 0 else 1 - col
        sib.append(send(pair_ref.at[:, :, which, 1 - core], pair_sib.at[:, rel],
                        sib_send.at[rel], sib_recv.at[rel], sibling))
    sib.append(send(left_hbm, left_sib, sib_send.at[2], sib_recv.at[2], sibling))
    for copy in sib:
        copy.start()

    load_right.wait()
    wide = right_ref[...].astype(F32)
    rows_f32[...] = jnp.concatenate([wide, wide], axis=0).T
    low = lax.broadcasted_iota(jnp.int32, (block, lanes), 1) < n_seq
    for ep in range(HALF):
        even = rows_f32[pl.ds(2 * ep, block, stride=C), :]
        odd = rows_f32[pl.ds(2 * ep + 1, block, stride=C), :]
        gathered[0, z, ep] = jnp.where(low, even, odd).astype(BF16)

    def nearest(k):
        both = jnp.minimum(z, depth - 1 - z)
        toward = jnp.where(z < depth - 1 - z, 1, -1)
        near = z + (k + 1) // 2 * (1 if k % 2 else -1)
        return jnp.where(k <= 2 * both, near, z + toward * (k - both))

    gather_z = []
    gather_y = [send(gathered.at[0, z], gathered.at[1, z],
                     agy_send.at[z], agy_recv.at[z], across)]
    arrive_z = []
    for k in range(1, depth):
        other = nearest(k)
        gather_z.append(send(gathered.at[0, z], gathered.at[0, z],
                             agz_send.at[other], agz_recv.at[z], at_z(other)))
        arrive_z.append(send(gathered.at[0, other], gathered.at[0, other],
                             agz_send.at[other], agz_recv.at[other], at_z(other)))
        gather_y.append(send(gathered.at[0, other], gathered.at[1, other],
                             agy_send.at[other], agy_recv.at[other], across))
    for copy in gather_z:
        copy.start()
    gather_y[0].start()

    load_weight.wait()
    weight_f32[...] = weight_ref[...].astype(F32)
    for e in range(C):
        weight_perm[e * C:(e + 1) * C, :] = weight_f32[pl.ds(e, C, stride=C), :].astype(BF16)

    rows_g = C // GROUPS * C
    grads = (grad_a, grad_b, grad_c, grad_d)

    def project(g, pair, first):
        taps = weight_perm[g * rows_g:(g + 1) * rows_g, :]

        def step(t, carry):
            slab = pair[pl.ds(2 * t, 2)].reshape(2 * width, -1)
            res = lax.dot_general(taps, slab, (((1,), (1,)), ((), ())),
                                  preferred_element_type=F32).astype(BF16)
            for k in range(2):
                row = first + (2 * t + k) * C
                if not isinstance(t, int):
                    row = pl.multiple_of(row, C)
                for q in range(C // GROUPS):
                    grads[g][pl.ds(row, C), q * width:(q + 1) * width] = (
                        res[q * C:(q + 1) * C, k * width:(k + 1) * width])
            return carry

        if width <= 128:
            for t in range(block // 2):
                step(t, 0)
        else:
            lax.fori_loop(0, block // 2, step, 0, unroll=2)

    reduce_y = [send(y_send.at[g], y_recv.at[g], rsy_send.at[g], rsy_recv.at[g], across)
                for g in range(GROUPS)]
    reduce_z = [
        [send(z_send.at[g, z_peer(d)], z_recv.at[g, d - 1],
              rsz_send.at[g, d - 1], rsz_recv.at[g, d - 1], at_z(z_peer(d)))
         for d in range(1, depth)]
        for g in range(GROUPS)
    ]

    def columns(g):
        res = jnp.dot(left_ref[...], grads[g][:chans, :], preferred_element_type=F32)
        res += jnp.dot(left_sib[...], grads[g][chans:, :], preferred_element_type=F32)
        for q in range(per_group):
            at = 2 * q * width
            turned = jnp.concatenate(
                [res[:, at:at + width], res[:, at + width:at + 2 * width]], axis=0).T
            where = slice(q * lanes, (q + 1) * lanes)
            column_sum[g, :, where] = turned[:span]
            y_send[g, :, where] = turned[span:].astype(BF16)

    def second(g):
        reduce_y[g].wait_recv()
        column_sum[g] += y_recv[g].astype(F32)
        for k in range(depth):
            z_send[g, k] = column_sum[g, k * block:(k + 1) * block, :].astype(BF16)
        for copy in reduce_z[g]:
            copy.start()

    def finish(g):
        acc = column_sum[g, pl.ds(pl.multiple_of(z * block, block), block), :]
        for d in range(1, depth):
            reduce_z[g][d - 1].wait_recv()
            acc += z_recv[g, d - 1].astype(F32)
        for q in range(per_group):
            ep = g * per_group + q
            tile = acc[:, q * lanes:(q + 1) * lanes] * (1.0 / n_seq)
            rows_f32[pl.ds(2 * ep, block, stride=C), :] = tile
            rows_f32[pl.ds(2 * ep + 1, block, stride=C), :] = pltpu.roll(tile, n_seq, 1)

    def rows(first):
        part = per_group * 2 * width
        acc = None
        for g in range(GROUPS):
            term = jnp.dot(grads[g][first:first + chans, :],
                           right_all[g * part:(g + 1) * part, :], preferred_element_type=F32)
            acc = term if acc is None else acc + term
        turned = acc.T
        return turned[:n_seq] + turned[n_seq:]

    for copy in loads:
        copy.wait()
    for g in range(GROUPS // 2):
        project(g, pair_own, 0)
    for copy in sib:
        copy.wait_recv()
    project(0, pair_sib, chans)
    for g in range(GROUPS):
        if g + 1 < GROUPS:
            if g + 1 >= GROUPS // 2:
                project(g + 1, pair_own, 0)
            project(g + 1, pair_sib, chans)
        columns(g)
        reduce_y[g].start()
        for d in range(1, depth):
            if max(1, (2 * d) // (depth - 1)) == g:
                arrive_z[d - 1].wait_recv()
                gather_y[d].start()
        if g >= 2:
            second(g - 2)

    for copy in gather_y:
        copy.wait_recv()
    upper = lax.broadcasted_iota(jnp.int32, (width, lanes), 1) >= n_seq
    mask_odd = upper.astype(F32).astype(BF16)
    mask_even = (1.0 - upper.astype(F32)).astype(BF16)
    for ep in range(HALF):
        piece = gathered[:, :, ep].reshape(width, lanes)
        right_all[2 * ep * width:(2 * ep + 1) * width, :] = piece * mask_even
        right_all[(2 * ep + 1) * width:(2 * ep + 2) * width, :] = piece * mask_odd

    left_send[...] = rows(chans)
    exchange = send(left_send, left_recv, sib_send.at[3], sib_recv.at[3], sibling)
    exchange.start()
    second(GROUPS - 2)
    second(GROUPS - 1)
    for g in range(GROUPS // 2):
        finish(g)
    mine = rows(0)
    exchange.wait_recv()
    out[0] = ((mine + left_recv[...]) * (1.0 / n_seq)).astype(BF16)

    for g in range(GROUPS // 2, GROUPS):
        finish(g)
    out[1] = rows_f32[...].T[:n_seq].astype(BF16)

    for copy in sib + gather_z + gather_y + reduce_y + [exchange]:
        copy.wait_send()
    for group in reduce_z:
        for copy in group:
            copy.wait_send()


def per_device(n_row, left_proj, right_proj, pair_cot, out_weight):
    n_seq = left_proj.shape[0]
    block, total, p_size = pair_cot.shape
    depth = n_row // (CORES * COLS)
    span = depth * block
    width = COLS * span
    chans = block * C
    lanes = 2 * n_seq
    group_lanes = HALF // GROUPS * lanes
    pair = pair_cot.reshape(block, depth, COLS, CORES, block, p_size)
    vmem = pl.BlockSpec(memory_space=pltpu.VMEM)
    dma = pltpu.SemaphoreType.DMA
    flops = 2 * block * total * C * C * (p_size + 2 * n_seq)
    scratch = [
        pltpu.VMEM(left_proj.shape, BF16),
        pltpu.VMEM(right_proj.shape, BF16),
        pltpu.VMEM(out_weight.shape, BF16),
        pltpu.VMEM((block, COLS, depth, block, p_size), BF16),
        pltpu.VMEM((block, COLS, depth, block, p_size), BF16),
        pltpu.VMEM((n_seq, chans), BF16),
        pltpu.VMEM((C * C, p_size), F32),
        pltpu.VMEM((C * C, p_size), BF16),
        *[pltpu.VMEM((2 * chans, C // GROUPS * width), BF16)] * GROUPS,
        pltpu.VMEM((chans, lanes), F32),
        pltpu.VMEM((COLS, depth, HALF, block, lanes), BF16),
        pltpu.VMEM((C * width, lanes), BF16),
        pltpu.VMEM((GROUPS, span, group_lanes), F32),
        pltpu.VMEM((GROUPS, span, group_lanes), BF16),
        pltpu.VMEM((GROUPS, span, group_lanes), BF16),
        pltpu.VMEM((GROUPS, depth, block, group_lanes), BF16),
        pltpu.VMEM((GROUPS, depth - 1, block, group_lanes), BF16),
        pltpu.VMEM((n_seq, chans), F32),
        pltpu.VMEM((n_seq, chans), F32),
        dma((COLS + 3,)),
        dma((4,)), dma((4,)),
        dma((depth,)), dma((depth,)),
        dma((depth,)), dma((depth,)),
        dma((GROUPS,)), dma((GROUPS,)),
        dma((GROUPS, depth - 1)), dma((GROUPS, depth - 1)),
    ]
    held = sum(2 * math.prod(b.shape) if b.dtype == BF16 else 4 * math.prod(b.shape)
               for b in scratch if b.dtype in (BF16, F32))
    held += 8 * left_proj.size
    sums = pl.pallas_call(
        functools.partial(kernel, depth, n_seq, block),
        out_shape=pltpu.VMEM((2, n_seq, chans), BF16),
        in_specs=[pl.BlockSpec(memory_space=pltpu.HBM)] * 4,
        out_specs=vmem,
        scratch_shapes=scratch,
        compiler_params=pltpu.CompilerParams(
            collective_id=0, has_side_effects=True, vmem_limit_bytes=held + 4 * 1024 * 1024
        ),
        cost_estimate=pl.CostEstimate(
            flops=flops, bytes_accessed=4 * pair_cot.size, transcendentals=0
        ),
    )(*[pltpu.with_memory_space_constraint(x, pltpu.HBM)
        for x in (left_proj, right_proj, pair, out_weight)])
    return (sums[0], sums[1])


def solution(mesh):
    return jax.shard_map(
        functools.partial(per_device, mesh.shape["row"]),
        mesh=mesh,
        in_specs=(P("groups", "row"), P("groups", "row"), P(("groups", "row"), None, None), P()),
        out_specs=(P("groups", "row"), P("groups", "row")),
        check_vma=False,
    )
```

```python
import functools
import math

import jax
import jax.numpy as jnp
from jax import lax
from jax.experimental import pallas as pl
from jax.experimental.pallas import tpu as pltpu
from jax.sharding import PartitionSpec as P

C = 32
CORES = 2
COLS = 2
HALF = C // 2
GROUPS = 4
MESH = pl.DeviceIdType.MESH
F32 = jnp.float32
BF16 = jnp.bfloat16


def kernel(
    depth, n_seq, block,
    left_hbm, right_hbm, pair_ref, weight_hbm,
    out,
    left_ref, right_ref, weight_ref,
    pair_own, pair_sib, left_sib, weight_f32, weight_perm, grad_a, grad_b, grad_c, grad_d, rows_f32,
    gathered, right_all, column_sum, y_send, y_recv, z_send, z_recv,
    left_send, left_recv,
    load_sem, sib_send, sib_recv, agz_send, agz_recv, agy_send, agy_recv,
    rsy_send, rsy_recv, rsz_send, rsz_recv,
):
    me = lax.axis_index("row")
    core = lax.rem(me, CORES)
    col = lax.rem(me // CORES, COLS)
    z = me // (CORES * COLS)
    sibling = me + 1 - 2 * core
    across = me + CORES * (1 - 2 * col)
    span = depth * block
    width = COLS * span
    chans = block * C
    lanes = 2 * n_seq
    per_group = HALF // GROUPS
    group_lanes = per_group * lanes

    def z_peer(step):
        return lax.rem(z + step, depth)

    def at_z(other):
        return other * (CORES * COLS) + lax.rem(me, CORES * COLS)

    def send(src, dst, s_sem, r_sem, target):
        return pltpu.make_async_remote_copy(
            src_ref=src, dst_ref=dst, send_sem=s_sem, recv_sem=r_sem,
            device_id={"row": target}, device_id_type=MESH,
        )

    barrier = pltpu.get_barrier_semaphore()
    for target in [sibling, across] + [at_z(z_peer(d)) for d in range(1, depth)]:
        pl.semaphore_signal(barrier, inc=1, device_id={"row": target}, device_id_type=MESH)

    load_right = pltpu.make_async_copy(right_hbm, right_ref, load_sem.at[COLS])
    load_weight = pltpu.make_async_copy(weight_hbm, weight_ref, load_sem.at[COLS + 1])
    load_left = pltpu.make_async_copy(left_hbm, left_ref, load_sem.at[COLS + 2])
    loads = [load_left]
    for rel in range(COLS):
        which = col if rel == 0 else 1 - col
        loads.append(pltpu.make_async_copy(
            pair_ref.at[:, :, which, core], pair_own.at[:, rel], load_sem.at[rel]))
    for copy in [load_right, load_weight] + loads:
        copy.start()

    pl.semaphore_wait(barrier, depth + 1)

    sib = []
    for rel in range(COLS):
        which = col if rel == 0 else 1 - col
        sib.append(send(pair_ref.at[:, :, which, 1 - core], pair_sib.at[:, rel],
                        sib_send.at[rel], sib_recv.at[rel], sibling))
    sib.append(send(left_hbm, left_sib, sib_send.at[2], sib_recv.at[2], sibling))
    for copy in sib:
        copy.start()

    load_right.wait()
    wide = right_ref[...].astype(F32)
    rows_f32[...] = jnp.concatenate([wide, wide], axis=0).T
    low = lax.broadcasted_iota(jnp.int32, (block, lanes), 1) < n_seq
    for ep in range(HALF):
        even = rows_f32[pl.ds(2 * ep, block, stride=C), :]
        odd = rows_f32[pl.ds(2 * ep + 1, block, stride=C), :]
        gathered[0, z, ep] = jnp.where(low, even, odd).astype(BF16)

    def nearest(k):
        both = jnp.minimum(z, depth - 1 - z)
        toward = jnp.where(z < depth - 1 - z, 1, -1)
        near = z + (k + 1) // 2 * (1 if k % 2 else -1)
        return jnp.where(k <= 2 * both, near, z + toward * (k - both))

    gather_z = []
    gather_y = [send(gathered.at[0, z], gathered.at[1, z],
                     agy_send.at[z], agy_recv.at[z], across)]
    arrive_z = []
    for k in range(1, depth):
        other = nearest(k)
        gather_z.append(send(gathered.at[0, z], gathered.at[0, z],
                             agz_send.at[other], agz_recv.at[z], at_z(other)))
        arrive_z.append(send(gathered.at[0, other], gathered.at[0, other],
                             agz_send.at[other], agz_recv.at[other], at_z(other)))
        gather_y.append(send(gathered.at[0, other], gathered.at[1, other],
                             agy_send.at[other], agy_recv.at[other], across))
    for copy in gather_z:
        copy.start()
    gather_y[0].start()

    load_weight.wait()
    weight_f32[...] = weight_ref[...].astype(F32)
    for e in range(C):
        weight_perm[e * C:(e + 1) * C, :] = weight_f32[pl.ds(e, C, stride=C), :].astype(BF16)

    grads = (grad_a, grad_b, grad_c, grad_d)
    per_grad = C // GROUPS

    def project(pair, first):
        def step(t, carry):
            slab = pair[pl.ds(2 * t, 2)].reshape(2 * width, -1)
            res = lax.dot_general(weight_perm[...], slab, (((1,), (1,)), ((), ())),
                                  preferred_element_type=F32).astype(BF16)
            for k in range(2):
                row = pl.multiple_of(first + (2 * t + k) * C, C)
                for e in range(C):
                    q = e % per_grad
                    grads[e // per_grad][pl.ds(row, C), q * width:(q + 1) * width] = (
                        res[e * C:(e + 1) * C, k * width:(k + 1) * width])
            return carry

        lax.fori_loop(0, block // 2, step, 0, unroll=2)

    reduce_y = [send(y_send.at[g], y_recv.at[g], rsy_send.at[g], rsy_recv.at[g], across)
                for g in range(GROUPS)]
    reduce_z = [
        [send(z_send.at[g, z_peer(d)], z_recv.at[g, d - 1],
              rsz_send.at[g, d - 1], rsz_recv.at[g, d - 1], at_z(z_peer(d)))
         for d in range(1, depth)]
        for g in range(GROUPS)
    ]

    def columns(g):
        res = jnp.dot(left_ref[...], grads[g][:chans, :], preferred_element_type=F32)
        res += jnp.dot(left_sib[...], grads[g][chans:, :], preferred_element_type=F32)
        for q in range(per_group):
            at = 2 * q * width
            turned = jnp.concatenate(
                [res[:, at:at + width], res[:, at + width:at + 2 * width]], axis=0).T
            where = slice(q * lanes, (q + 1) * lanes)
            column_sum[g, :, where] = turned[:span]
            y_send[g, :, where] = turned[span:].astype(BF16)

    def second(g):
        reduce_y[g].wait_recv()
        column_sum[g] += y_recv[g].astype(F32)
        for k in range(depth):
            z_send[g, k] = column_sum[g, k * block:(k + 1) * block, :].astype(BF16)
        for copy in reduce_z[g]:
            copy.start()

    def finish(g):
        acc = column_sum[g, pl.ds(pl.multiple_of(z * block, block), block), :]
        for d in range(1, depth):
            reduce_z[g][d - 1].wait_recv()
            acc += z_recv[g, d - 1].astype(F32)
        for q in range(per_group):
            ep = g * per_group + q
            tile = acc[:, q * lanes:(q + 1) * lanes] * (1.0 / n_seq)
            rows_f32[pl.ds(2 * ep, block, stride=C), :] = tile
            rows_f32[pl.ds(2 * ep + 1, block, stride=C), :] = pltpu.roll(tile, n_seq, 1)

    def rows(first):
        part = per_group * 2 * width
        acc = None
        for g in range(GROUPS):
            term = jnp.dot(grads[g][first:first + chans, :],
                           right_all[g * part:(g + 1) * part, :], preferred_element_type=F32)
            acc = term if acc is None else acc + term
        turned = acc.T
        return turned[:n_seq] + turned[n_seq:]

    for copy in loads:
        copy.wait()
    project(pair_own, 0)
    for copy in sib:
        copy.wait_recv()
    project(pair_sib, chans)
    for k in range(1, depth):
        arrive_z[k - 1].wait_recv()
        gather_y[k].start()
    for g in range(GROUPS):
        columns(g)
        reduce_y[g].start()
        if g >= 2:
            second(g - 2)

    for copy in gather_y:
        copy.wait_recv()
    upper = lax.broadcasted_iota(jnp.int32, (width, lanes), 1) >= n_seq
    mask_odd = upper.astype(F32).astype(BF16)
    mask_even = (1.0 - upper.astype(F32)).astype(BF16)
    for ep in range(HALF):
        piece = gathered[:, :, ep].reshape(width, lanes)
        right_all[2 * ep * width:(2 * ep + 1) * width, :] = piece * mask_even
        right_all[(2 * ep + 1) * width:(2 * ep + 2) * width, :] = piece * mask_odd

    left_send[...] = rows(chans)
    exchange = send(left_send, left_recv, sib_send.at[3], sib_recv.at[3], sibling)
    exchange.start()
    second(GROUPS - 2)
    second(GROUPS - 1)
    for g in range(GROUPS // 2):
        finish(g)
    mine = rows(0)
    exchange.wait_recv()
    out[0] = ((mine + left_recv[...]) * (1.0 / n_seq)).astype(BF16)

    for g in range(GROUPS // 2, GROUPS):
        finish(g)
    out[1] = rows_f32[...].T[:n_seq].astype(BF16)

    for copy in sib + gather_z + gather_y + reduce_y + [exchange]:
        copy.wait_send()
    for group in reduce_z:
        for copy in group:
            copy.wait_send()


def per_device(n_row, left_proj, right_proj, pair_cot, out_weight):
    n_seq = left_proj.shape[0]
    block, total, p_size = pair_cot.shape
    depth = n_row // (CORES * COLS)
    span = depth * block
    width = COLS * span
    chans = block * C
    lanes = 2 * n_seq
    group_lanes = HALF // GROUPS * lanes
    pair = pair_cot.reshape(block, depth, COLS, CORES, block, p_size)
    vmem = pl.BlockSpec(memory_space=pltpu.VMEM)
    dma = pltpu.SemaphoreType.DMA
    flops = 2 * block * total * C * C * (p_size + 2 * n_seq)
    scratch = [
        pltpu.VMEM(left_proj.shape, BF16),
        pltpu.VMEM(right_proj.shape, BF16),
        pltpu.VMEM(out_weight.shape, BF16),
        pltpu.VMEM((block, COLS, depth, block, p_size), BF16),
        pltpu.VMEM((block, COLS, depth, block, p_size), BF16),
        pltpu.VMEM((n_seq, chans), BF16),
        pltpu.VMEM((C * C, p_size), F32),
        pltpu.VMEM((C * C, p_size), BF16),
        *[pltpu.VMEM((2 * chans, C // GROUPS * width), BF16)] * GROUPS,
        pltpu.VMEM((chans, lanes), F32),
        pltpu.VMEM((COLS, depth, HALF, block, lanes), BF16),
        pltpu.VMEM((C * width, lanes), BF16),
        pltpu.VMEM((GROUPS, span, group_lanes), F32),
        pltpu.VMEM((GROUPS, span, group_lanes), BF16),
        pltpu.VMEM((GROUPS, span, group_lanes), BF16),
        pltpu.VMEM((GROUPS, depth, block, group_lanes), BF16),
        pltpu.VMEM((GROUPS, depth - 1, block, group_lanes), BF16),
        pltpu.VMEM((n_seq, chans), F32),
        pltpu.VMEM((n_seq, chans), F32),
        dma((COLS + 3,)),
        dma((4,)), dma((4,)),
        dma((depth,)), dma((depth,)),
        dma((depth,)), dma((depth,)),
        dma((GROUPS,)), dma((GROUPS,)),
        dma((GROUPS, depth - 1)), dma((GROUPS, depth - 1)),
    ]
    held = sum(2 * math.prod(b.shape) if b.dtype == BF16 else 4 * math.prod(b.shape)
               for b in scratch if b.dtype in (BF16, F32))
    held += 8 * left_proj.size
    sums = pl.pallas_call(
        functools.partial(kernel, depth, n_seq, block),
        out_shape=pltpu.VMEM((2, n_seq, chans), BF16),
        in_specs=[pl.BlockSpec(memory_space=pltpu.HBM)] * 4,
        out_specs=vmem,
        scratch_shapes=scratch,
        compiler_params=pltpu.CompilerParams(
            collective_id=0, has_side_effects=True, vmem_limit_bytes=held + 4 * 1024 * 1024
        ),
        cost_estimate=pl.CostEstimate(
            flops=flops, bytes_accessed=4 * pair_cot.size, transcendentals=0
        ),
    )(*[pltpu.with_memory_space_constraint(x, pltpu.HBM)
        for x in (left_proj, right_proj, pair, out_weight)])
    return (sums[0], sums[1])


def solution(mesh):
    return jax.shard_map(
        functools.partial(per_device, mesh.shape["row"]),
        mesh=mesh,
        in_specs=(P("groups", "row"), P("groups", "row"), P(("groups", "row"), None, None), P()),
        out_specs=(P("groups", "row"), P("groups", "row")),
        check_vma=False,
    )
```

```python
import functools
import math

import jax
import jax.numpy as jnp
from jax import lax
from jax.experimental import pallas as pl
from jax.experimental.pallas import tpu as pltpu
from jax.sharding import PartitionSpec as P

C = 32
CORES = 2
COLS = 2
HALF = C // 2
GROUPS = 4
MESH = pl.DeviceIdType.MESH
F32 = jnp.float32
BF16 = jnp.bfloat16


def kernel(
    depth, n_seq, block,
    left_hbm, right_hbm, pair_ref, weight_hbm,
    out,
    left_ref, right_ref, weight_ref,
    pair_own, pair_sib, left_sib, weight_f32, weight_perm, grad_a, grad_b, grad_c, grad_d, rows_f32,
    gathered, right_all, column_sum, y_send, y_recv, z_send, z_recv,
    left_send, left_recv,
    load_sem, sib_send, sib_recv, agz_send, agz_recv, agy_send, agy_recv,
    rsy_send, rsy_recv, rsz_send, rsz_recv,
):
    me = lax.axis_index("row")
    core = lax.rem(me, CORES)
    col = lax.rem(me // CORES, COLS)
    z = me // (CORES * COLS)
    sibling = me + 1 - 2 * core
    across = me + CORES * (1 - 2 * col)
    span = depth * block
    width = COLS * span
    chans = block * C
    lanes = 2 * n_seq
    per_group = HALF // GROUPS
    group_lanes = per_group * lanes

    def z_peer(step):
        return lax.rem(z + step, depth)

    def at_z(other):
        return other * (CORES * COLS) + lax.rem(me, CORES * COLS)

    def send(src, dst, s_sem, r_sem, target):
        return pltpu.make_async_remote_copy(
            src_ref=src, dst_ref=dst, send_sem=s_sem, recv_sem=r_sem,
            device_id={"row": target}, device_id_type=MESH,
        )

    barrier = pltpu.get_barrier_semaphore()
    for target in [sibling, across] + [at_z(z_peer(d)) for d in range(1, depth)]:
        pl.semaphore_signal(barrier, inc=1, device_id={"row": target}, device_id_type=MESH)

    load_right = pltpu.make_async_copy(right_hbm, right_ref, load_sem.at[COLS])
    load_weight = pltpu.make_async_copy(weight_hbm, weight_ref, load_sem.at[COLS + 1])
    load_left = pltpu.make_async_copy(left_hbm, left_ref, load_sem.at[COLS + 2])
    loads = [load_left]
    for rel in range(COLS):
        which = col if rel == 0 else 1 - col
        loads.append(pltpu.make_async_copy(
            pair_ref.at[:, :, which, core], pair_own.at[:, rel], load_sem.at[rel]))
    for copy in [load_right, load_weight] + loads:
        copy.start()

    pl.semaphore_wait(barrier, depth + 1)

    sib = []
    for rel in range(COLS):
        which = col if rel == 0 else 1 - col
        sib.append(send(pair_ref.at[:, :, which, 1 - core], pair_sib.at[:, rel],
                        sib_send.at[rel], sib_recv.at[rel], sibling))
    sib.append(send(left_hbm, left_sib, sib_send.at[2], sib_recv.at[2], sibling))
    for copy in sib:
        copy.start()

    load_right.wait()
    wide = right_ref[...].astype(F32)
    rows_f32[...] = jnp.concatenate([wide, wide], axis=0).T
    low = lax.broadcasted_iota(jnp.int32, (block, lanes), 1) < n_seq
    for ep in range(HALF):
        even = rows_f32[pl.ds(2 * ep, block, stride=C), :]
        odd = rows_f32[pl.ds(2 * ep + 1, block, stride=C), :]
        gathered[0, z, ep] = jnp.where(low, even, odd).astype(BF16)

    def nearest(k):
        both = jnp.minimum(z, depth - 1 - z)
        toward = jnp.where(z < depth - 1 - z, 1, -1)
        near = z + (k + 1) // 2 * (1 if k % 2 else -1)
        return jnp.where(k <= 2 * both, near, z + toward * (k - both))

    gather_z = []
    gather_y = [send(gathered.at[0, z], gathered.at[1, z],
                     agy_send.at[z], agy_recv.at[z], across)]
    arrive_z = []
    for k in range(1, depth):
        other = nearest(k)
        gather_z.append(send(gathered.at[0, z], gathered.at[0, z],
                             agz_send.at[other], agz_recv.at[z], at_z(other)))
        arrive_z.append(send(gathered.at[0, other], gathered.at[0, other],
                             agz_send.at[other], agz_recv.at[other], at_z(other)))
        gather_y.append(send(gathered.at[0, other], gathered.at[1, other],
                             agy_send.at[other], agy_recv.at[other], across))
    for copy in gather_z:
        copy.start()
    gather_y[0].start()

    load_weight.wait()
    weight_f32[...] = weight_ref[...].astype(F32)
    for e in range(C):
        weight_perm[e * C:(e + 1) * C, :] = weight_f32[pl.ds(e, C, stride=C), :].astype(BF16)

    grads = (grad_a, grad_b, grad_c, grad_d)
    per_grad = C // GROUPS

    def project(pair, first, groups):
        taps = slice(groups[0] * per_grad * C, (groups[-1] + 1) * per_grad * C)

        def step(t, carry):
            slab = pair[pl.ds(2 * t, 2)].reshape(2 * width, -1)
            res = lax.dot_general(weight_perm[taps, :], slab, (((1,), (1,)), ((), ())),
                                  preferred_element_type=F32).astype(BF16)
            for k in range(2):
                row = pl.multiple_of(first + (2 * t + k) * C, C)
                for e in range(len(groups) * per_grad):
                    q = e % per_grad
                    grads[groups[e // per_grad]][pl.ds(row, C), q * width:(q + 1) * width] = (
                        res[e * C:(e + 1) * C, k * width:(k + 1) * width])
            return carry

        lax.fori_loop(0, block // 2, step, 0, unroll=2 if len(groups) > 1 else 4)

    reduce_y = [send(y_send.at[g], y_recv.at[g], rsy_send.at[g], rsy_recv.at[g], across)
                for g in range(GROUPS)]
    reduce_z = [
        [send(z_send.at[g, z_peer(d)], z_recv.at[g, d - 1],
              rsz_send.at[g, d - 1], rsz_recv.at[g, d - 1], at_z(z_peer(d)))
         for d in range(1, depth)]
        for g in range(GROUPS)
    ]

    def columns(g):
        res = jnp.dot(left_ref[...], grads[g][:chans, :], preferred_element_type=F32)
        res += jnp.dot(left_sib[...], grads[g][chans:, :], preferred_element_type=F32)
        for q in range(per_group):
            at = 2 * q * width
            turned = jnp.concatenate(
                [res[:, at:at + width], res[:, at + width:at + 2 * width]], axis=0).T
            where = slice(q * lanes, (q + 1) * lanes)
            column_sum[g, :, where] = turned[:span]
            y_send[g, :, where] = turned[span:].astype(BF16)

    def second(g):
        reduce_y[g].wait_recv()
        column_sum[g] += y_recv[g].astype(F32)
        for k in range(depth):
            z_send[g, k] = column_sum[g, k * block:(k + 1) * block, :].astype(BF16)
        for copy in reduce_z[g]:
            copy.start()

    def finish(g):
        acc = column_sum[g, pl.ds(pl.multiple_of(z * block, block), block), :]
        for d in range(1, depth):
            reduce_z[g][d - 1].wait_recv()
            acc += z_recv[g, d - 1].astype(F32)
        for q in range(per_group):
            ep = g * per_group + q
            tile = acc[:, q * lanes:(q + 1) * lanes] * (1.0 / n_seq)
            rows_f32[pl.ds(2 * ep, block, stride=C), :] = tile
            rows_f32[pl.ds(2 * ep + 1, block, stride=C), :] = pltpu.roll(tile, n_seq, 1)

    def rows(first):
        part = per_group * 2 * width
        acc = None
        for g in range(GROUPS):
            term = jnp.dot(grads[g][first:first + chans, :],
                           right_all[g * part:(g + 1) * part, :], preferred_element_type=F32)
            acc = term if acc is None else acc + term
        turned = acc.T
        return turned[:n_seq] + turned[n_seq:]

    for copy in loads:
        copy.wait()
    project(pair_own, 0, tuple(range(GROUPS)))
    for copy in sib:
        copy.wait_recv()
    for g in range(GROUPS):
        project(pair_sib, chans, (g,))
        columns(g)
        reduce_y[g].start()
        for k in range(1, depth):
            if (2 * (k - 1) + 1) // (depth - 1) == g:
                arrive_z[k - 1].wait_recv()
                gather_y[k].start()
        if g >= 2:
            second(g - 2)

    for copy in gather_y:
        copy.wait_recv()
    upper = lax.broadcasted_iota(jnp.int32, (width, lanes), 1) >= n_seq
    mask_odd = upper.astype(F32).astype(BF16)
    mask_even = (1.0 - upper.astype(F32)).astype(BF16)
    for ep in range(HALF):
        piece = gathered[:, :, ep].reshape(width, lanes)
        right_all[2 * ep * width:(2 * ep + 1) * width, :] = piece * mask_even
        right_all[(2 * ep + 1) * width:(2 * ep + 2) * width, :] = piece * mask_odd

    left_send[...] = rows(chans)
    exchange = send(left_send, left_recv, sib_send.at[3], sib_recv.at[3], sibling)
    exchange.start()
    second(GROUPS - 2)
    second(GROUPS - 1)
    for g in range(GROUPS // 2):
        finish(g)
    mine = rows(0)
    exchange.wait_recv()
    out[0] = ((mine + left_recv[...]) * (1.0 / n_seq)).astype(BF16)

    for g in range(GROUPS // 2, GROUPS):
        finish(g)
    out[1] = rows_f32[...].T[:n_seq].astype(BF16)

    for copy in sib + gather_z + gather_y + reduce_y + [exchange]:
        copy.wait_send()
    for group in reduce_z:
        for copy in group:
            copy.wait_send()


def per_device(n_row, left_proj, right_proj, pair_cot, out_weight):
    n_seq = left_proj.shape[0]
    block, total, p_size = pair_cot.shape
    depth = n_row // (CORES * COLS)
    span = depth * block
    width = COLS * span
    chans = block * C
    lanes = 2 * n_seq
    group_lanes = HALF // GROUPS * lanes
    pair = pair_cot.reshape(block, depth, COLS, CORES, block, p_size)
    vmem = pl.BlockSpec(memory_space=pltpu.VMEM)
    dma = pltpu.SemaphoreType.DMA
    flops = 2 * block * total * C * C * (p_size + 2 * n_seq)
    scratch = [
        pltpu.VMEM(left_proj.shape, BF16),
        pltpu.VMEM(right_proj.shape, BF16),
        pltpu.VMEM(out_weight.shape, BF16),
        pltpu.VMEM((block, COLS, depth, block, p_size), BF16),
        pltpu.VMEM((block, COLS, depth, block, p_size), BF16),
        pltpu.VMEM((n_seq, chans), BF16),
        pltpu.VMEM((C * C, p_size), F32),
        pltpu.VMEM((C * C, p_size), BF16),
        *[pltpu.VMEM((2 * chans, C // GROUPS * width), BF16)] * GROUPS,
        pltpu.VMEM((chans, lanes), F32),
        pltpu.VMEM((COLS, depth, HALF, block, lanes), BF16),
        pltpu.VMEM((C * width, lanes), BF16),
        pltpu.VMEM((GROUPS, span, group_lanes), F32),
        pltpu.VMEM((GROUPS, span, group_lanes), BF16),
        pltpu.VMEM((GROUPS, span, group_lanes), BF16),
        pltpu.VMEM((GROUPS, depth, block, group_lanes), BF16),
        pltpu.VMEM((GROUPS, depth - 1, block, group_lanes), BF16),
        pltpu.VMEM((n_seq, chans), F32),
        pltpu.VMEM((n_seq, chans), F32),
        dma((COLS + 3,)),
        dma((4,)), dma((4,)),
        dma((depth,)), dma((depth,)),
        dma((depth,)), dma((depth,)),
        dma((GROUPS,)), dma((GROUPS,)),
        dma((GROUPS, depth - 1)), dma((GROUPS, depth - 1)),
    ]
    held = sum(2 * math.prod(b.shape) if b.dtype == BF16 else 4 * math.prod(b.shape)
               for b in scratch if b.dtype in (BF16, F32))
    held += 8 * left_proj.size
    sums = pl.pallas_call(
        functools.partial(kernel, depth, n_seq, block),
        out_shape=pltpu.VMEM((2, n_seq, chans), BF16),
        in_specs=[pl.BlockSpec(memory_space=pltpu.HBM)] * 4,
        out_specs=vmem,
        scratch_shapes=scratch,
        compiler_params=pltpu.CompilerParams(
            collective_id=0, has_side_effects=True, vmem_limit_bytes=held + 4 * 1024 * 1024
        ),
        cost_estimate=pl.CostEstimate(
            flops=flops, bytes_accessed=4 * pair_cot.size, transcendentals=0
        ),
    )(*[pltpu.with_memory_space_constraint(x, pltpu.HBM)
        for x in (left_proj, right_proj, pair, out_weight)])
    return (sums[0], sums[1])


def solution(mesh):
    return jax.shard_map(
        functools.partial(per_device, mesh.shape["row"]),
        mesh=mesh,
        in_specs=(P("groups", "row"), P("groups", "row"), P(("groups", "row"), None, None), P()),
        out_specs=(P("groups", "row"), P("groups", "row")),
        check_vma=False,
    )
```

```python
import functools
import math

import jax
import jax.numpy as jnp
from jax import lax
from jax.experimental import pallas as pl
from jax.experimental.pallas import tpu as pltpu
from jax.sharding import PartitionSpec as P

C = 32
CORES = 2
COLS = 2
HALF = C // 2
GROUPS = 4
MESH = pl.DeviceIdType.MESH
F32 = jnp.float32
BF16 = jnp.bfloat16


def kernel(
    depth, n_seq, block,
    left_hbm, right_hbm, pair_ref, weight_hbm,
    out,
    left_ref, right_ref, weight_ref,
    pair_own, pair_sib, left_sib, weight_f32, weight_perm, grad_a, grad_b, grad_c, grad_d, rows_f32,
    gathered, right_all, column_sum, y_send, y_recv, z_send, z_recv,
    left_send, left_recv,
    load_sem, sib_send, sib_recv, agz_send, agz_recv, agy_send, agy_recv,
    rsy_send, rsy_recv, rsz_send, rsz_recv,
):
    me = lax.axis_index("row")
    core = lax.rem(me, CORES)
    col = lax.rem(me // CORES, COLS)
    z = me // (CORES * COLS)
    sibling = me + 1 - 2 * core
    across = me + CORES * (1 - 2 * col)
    span = depth * block
    width = COLS * span
    chans = block * C
    lanes = 2 * n_seq
    per_group = HALF // GROUPS
    group_lanes = per_group * lanes

    def z_peer(step):
        return lax.rem(z + step, depth)

    def at_z(other):
        return other * (CORES * COLS) + lax.rem(me, CORES * COLS)

    def send(src, dst, s_sem, r_sem, target):
        return pltpu.make_async_remote_copy(
            src_ref=src, dst_ref=dst, send_sem=s_sem, recv_sem=r_sem,
            device_id={"row": target}, device_id_type=MESH,
        )

    barrier = pltpu.get_barrier_semaphore()
    for target in [sibling, across] + [at_z(z_peer(d)) for d in range(1, depth)]:
        pl.semaphore_signal(barrier, inc=1, device_id={"row": target}, device_id_type=MESH)

    load_right = pltpu.make_async_copy(right_hbm, right_ref, load_sem.at[COLS])
    load_weight = pltpu.make_async_copy(weight_hbm, weight_ref, load_sem.at[COLS + 1])
    load_left = pltpu.make_async_copy(left_hbm, left_ref, load_sem.at[COLS + 2])
    loads = [load_left]
    for rel in range(COLS):
        which = col if rel == 0 else 1 - col
        loads.append(pltpu.make_async_copy(
            pair_ref.at[:, :, which, core], pair_own.at[:, rel], load_sem.at[rel]))
    for copy in [load_right, load_weight] + loads:
        copy.start()

    load_right.wait()
    wide = right_ref[...].astype(F32)
    rows_f32[...] = jnp.concatenate([wide, wide], axis=0).T
    low = lax.broadcasted_iota(jnp.int32, (block, lanes), 1) < n_seq
    for ep in range(HALF):
        even = rows_f32[pl.ds(2 * ep, block, stride=C), :]
        odd = rows_f32[pl.ds(2 * ep + 1, block, stride=C), :]
        gathered[0, z, ep] = jnp.where(low, even, odd).astype(BF16)

    pl.semaphore_wait(barrier, depth + 1)

    sib = []
    for rel in range(COLS):
        which = col if rel == 0 else 1 - col
        sib.append(send(pair_ref.at[:, :, which, 1 - core], pair_sib.at[:, rel],
                        sib_send.at[rel], sib_recv.at[rel], sibling))
    sib.append(send(left_hbm, left_sib, sib_send.at[2], sib_recv.at[2], sibling))
    def nearest(k):
        both = jnp.minimum(z, depth - 1 - z)
        toward = jnp.where(z < depth - 1 - z, 1, -1)
        near = z + (k + 1) // 2 * (1 if k % 2 else -1)
        return jnp.where(k <= 2 * both, near, z + toward * (k - both))

    gather_z = []
    gather_y = [send(gathered.at[0, z], gathered.at[1, z],
                     agy_send.at[z], agy_recv.at[z], across)]
    arrive_z = []
    for k in range(1, depth):
        other = nearest(k)
        gather_z.append(send(gathered.at[0, z], gathered.at[0, z],
                             agz_send.at[other], agz_recv.at[z], at_z(other)))
        arrive_z.append(send(gathered.at[0, other], gathered.at[0, other],
                             agz_send.at[other], agz_recv.at[other], at_z(other)))
        gather_y.append(send(gathered.at[0, other], gathered.at[1, other],
                             agy_send.at[other], agy_recv.at[other], across))
    for copy in gather_z:
        copy.start()
    gather_y[0].start()
    for copy in sib:
        copy.start()

    load_weight.wait()
    weight_f32[...] = weight_ref[...].astype(F32)
    for e in range(C):
        weight_perm[e * C:(e + 1) * C, :] = weight_f32[pl.ds(e, C, stride=C), :].astype(BF16)

    grads = (grad_a, grad_b, grad_c, grad_d)
    per_grad = C // GROUPS

    def project(pair, first, groups):
        taps = slice(groups[0] * per_grad * C, (groups[-1] + 1) * per_grad * C)

        def step(t, carry):
            slab = pair[pl.ds(2 * t, 2)].reshape(2 * width, -1)
            res = lax.dot_general(weight_perm[taps, :], slab, (((1,), (1,)), ((), ())),
                                  preferred_element_type=F32).astype(BF16)
            for k in range(2):
                row = pl.multiple_of(first + (2 * t + k) * C, C)
                for e in range(len(groups) * per_grad):
                    q = e % per_grad
                    grads[groups[e // per_grad]][pl.ds(row, C), q * width:(q + 1) * width] = (
                        res[e * C:(e + 1) * C, k * width:(k + 1) * width])
            return carry

        lax.fori_loop(0, block // 2, step, 0, unroll=2 if len(groups) > 1 else 4)

    reduce_y = [send(y_send.at[g], y_recv.at[g], rsy_send.at[g], rsy_recv.at[g], across)
                for g in range(GROUPS)]
    reduce_z = [
        [send(z_send.at[g, z_peer(d)], z_recv.at[g, d - 1],
              rsz_send.at[g, d - 1], rsz_recv.at[g, d - 1], at_z(z_peer(d)))
         for d in range(1, depth)]
        for g in range(GROUPS)
    ]

    def columns(g):
        res = jnp.dot(left_ref[...], grads[g][:chans, :], preferred_element_type=F32)
        res += jnp.dot(left_sib[...], grads[g][chans:, :], preferred_element_type=F32)
        for q in range(per_group):
            at = 2 * q * width
            turned = jnp.concatenate(
                [res[:, at:at + width], res[:, at + width:at + 2 * width]], axis=0).T
            where = slice(q * lanes, (q + 1) * lanes)
            column_sum[g, :, where] = turned[:span]
            y_send[g, :, where] = turned[span:].astype(BF16)

    def second(g):
        reduce_y[g].wait_recv()
        column_sum[g] += y_recv[g].astype(F32)
        for k in range(depth):
            z_send[g, k] = column_sum[g, k * block:(k + 1) * block, :].astype(BF16)
        for copy in reduce_z[g]:
            copy.start()

    def finish(g):
        acc = column_sum[g, pl.ds(pl.multiple_of(z * block, block), block), :]
        for d in range(1, depth):
            reduce_z[g][d - 1].wait_recv()
            acc += z_recv[g, d - 1].astype(F32)
        for q in range(per_group):
            ep = g * per_group + q
            tile = acc[:, q * lanes:(q + 1) * lanes] * (1.0 / n_seq)
            rows_f32[pl.ds(2 * ep, block, stride=C), :] = tile
            rows_f32[pl.ds(2 * ep + 1, block, stride=C), :] = pltpu.roll(tile, n_seq, 1)

    def rows(first):
        part = per_group * 2 * width
        acc = None
        for g in range(GROUPS):
            term = jnp.dot(grads[g][first:first + chans, :],
                           right_all[g * part:(g + 1) * part, :], preferred_element_type=F32)
            acc = term if acc is None else acc + term
        turned = acc.T
        return turned[:n_seq] + turned[n_seq:]

    for copy in loads:
        copy.wait()
    project(pair_own, 0, tuple(range(GROUPS)))
    for copy in sib:
        copy.wait_recv()
    for g in range(GROUPS):
        project(pair_sib, chans, (g,))
        columns(g)
        reduce_y[g].start()
        for k in range(1, depth):
            if (2 * (k - 1) + 1) // (depth - 1) == g:
                arrive_z[k - 1].wait_recv()
                gather_y[k].start()
        if g >= 2:
            second(g - 2)

    for copy in gather_y:
        copy.wait_recv()
    upper = lax.broadcasted_iota(jnp.int32, (width, lanes), 1) >= n_seq
    mask_odd = upper.astype(F32).astype(BF16)
    mask_even = (1.0 - upper.astype(F32)).astype(BF16)
    for ep in range(HALF):
        piece = gathered[:, :, ep].reshape(width, lanes)
        right_all[2 * ep * width:(2 * ep + 1) * width, :] = piece * mask_even
        right_all[(2 * ep + 1) * width:(2 * ep + 2) * width, :] = piece * mask_odd

    left_send[...] = rows(chans)
    exchange = send(left_send, left_recv, sib_send.at[3], sib_recv.at[3], sibling)
    exchange.start()
    second(GROUPS - 2)
    second(GROUPS - 1)
    for g in range(GROUPS // 2):
        finish(g)
    mine = rows(0)
    exchange.wait_recv()
    out[0] = ((mine + left_recv[...]) * (1.0 / n_seq)).astype(BF16)

    for g in range(GROUPS // 2, GROUPS):
        finish(g)
    out[1] = rows_f32[...].T[:n_seq].astype(BF16)

    for copy in sib + gather_z + gather_y + reduce_y + [exchange]:
        copy.wait_send()
    for group in reduce_z:
        for copy in group:
            copy.wait_send()


def per_device(n_row, left_proj, right_proj, pair_cot, out_weight):
    n_seq = left_proj.shape[0]
    block, total, p_size = pair_cot.shape
    depth = n_row // (CORES * COLS)
    span = depth * block
    width = COLS * span
    chans = block * C
    lanes = 2 * n_seq
    group_lanes = HALF // GROUPS * lanes
    pair = pair_cot.reshape(block, depth, COLS, CORES, block, p_size)
    vmem = pl.BlockSpec(memory_space=pltpu.VMEM)
    dma = pltpu.SemaphoreType.DMA
    flops = 2 * block * total * C * C * (p_size + 2 * n_seq)
    scratch = [
        pltpu.VMEM(left_proj.shape, BF16),
        pltpu.VMEM(right_proj.shape, BF16),
        pltpu.VMEM(out_weight.shape, BF16),
        pltpu.VMEM((block, COLS, depth, block, p_size), BF16),
        pltpu.VMEM((block, COLS, depth, block, p_size), BF16),
        pltpu.VMEM((n_seq, chans), BF16),
        pltpu.VMEM((C * C, p_size), F32),
        pltpu.VMEM((C * C, p_size), BF16),
        *[pltpu.VMEM((2 * chans, C // GROUPS * width), BF16)] * GROUPS,
        pltpu.VMEM((chans, lanes), F32),
        pltpu.VMEM((COLS, depth, HALF, block, lanes), BF16),
        pltpu.VMEM((C * width, lanes), BF16),
        pltpu.VMEM((GROUPS, span, group_lanes), F32),
        pltpu.VMEM((GROUPS, span, group_lanes), BF16),
        pltpu.VMEM((GROUPS, span, group_lanes), BF16),
        pltpu.VMEM((GROUPS, depth, block, group_lanes), BF16),
        pltpu.VMEM((GROUPS, depth - 1, block, group_lanes), BF16),
        pltpu.VMEM((n_seq, chans), F32),
        pltpu.VMEM((n_seq, chans), F32),
        dma((COLS + 3,)),
        dma((4,)), dma((4,)),
        dma((depth,)), dma((depth,)),
        dma((depth,)), dma((depth,)),
        dma((GROUPS,)), dma((GROUPS,)),
        dma((GROUPS, depth - 1)), dma((GROUPS, depth - 1)),
    ]
    held = sum(2 * math.prod(b.shape) if b.dtype == BF16 else 4 * math.prod(b.shape)
               for b in scratch if b.dtype in (BF16, F32))
    held += 8 * left_proj.size
    sums = pl.pallas_call(
        functools.partial(kernel, depth, n_seq, block),
        out_shape=pltpu.VMEM((2, n_seq, chans), BF16),
        in_specs=[pl.BlockSpec(memory_space=pltpu.HBM)] * 4,
        out_specs=vmem,
        scratch_shapes=scratch,
        compiler_params=pltpu.CompilerParams(
            collective_id=0, has_side_effects=True, vmem_limit_bytes=held + 4 * 1024 * 1024
        ),
        cost_estimate=pl.CostEstimate(
            flops=flops, bytes_accessed=4 * pair_cot.size, transcendentals=0
        ),
    )(*[pltpu.with_memory_space_constraint(x, pltpu.HBM)
        for x in (left_proj, right_proj, pair, out_weight)])
    return (sums[0], sums[1])


def solution(mesh):
    return jax.shard_map(
        functools.partial(per_device, mesh.shape["row"]),
        mesh=mesh,
        in_specs=(P("groups", "row"), P("groups", "row"), P(("groups", "row"), None, None), P()),
        out_specs=(P("groups", "row"), P("groups", "row")),
        check_vma=False,
    )
```

```python
import functools
import math

import jax
import jax.numpy as jnp
from jax import lax
from jax.experimental import pallas as pl
from jax.experimental.pallas import tpu as pltpu
from jax.sharding import PartitionSpec as P

C = 32
CORES = 2
COLS = 2
HALF = C // 2
GROUPS = 4
MESH = pl.DeviceIdType.MESH
F32 = jnp.float32
BF16 = jnp.bfloat16


def kernel(
    depth, n_seq, block,
    left_hbm, right_hbm, pair_ref, weight_hbm,
    out,
    left_ref, right_ref, weight_ref,
    pair_own, pair_sib, left_sib, weight_f32, weight_perm, grad_a, grad_b, grad_c, grad_d, rows_f32,
    gathered, right_all, column_sum, y_send, y_recv, z_send, z_recv,
    left_send, left_recv,
    load_sem, sib_send, sib_recv, agz_send, agz_recv, agy_send, agy_recv,
    rsy_send, rsy_recv, rsz_send, rsz_recv,
):
    me = lax.axis_index("row")
    core = lax.rem(me, CORES)
    col = lax.rem(me // CORES, COLS)
    z = me // (CORES * COLS)
    sibling = me + 1 - 2 * core
    across = me + CORES * (1 - 2 * col)
    span = depth * block
    width = COLS * span
    chans = block * C
    lanes = 2 * n_seq
    per_group = HALF // GROUPS
    group_lanes = per_group * lanes

    def z_peer(step):
        return lax.rem(z + step, depth)

    def at_z(other):
        return other * (CORES * COLS) + lax.rem(me, CORES * COLS)

    def send(src, dst, s_sem, r_sem, target):
        return pltpu.make_async_remote_copy(
            src_ref=src, dst_ref=dst, send_sem=s_sem, recv_sem=r_sem,
            device_id={"row": target}, device_id_type=MESH,
        )

    barrier = pltpu.get_barrier_semaphore()
    for target in [sibling, across] + [at_z(z_peer(d)) for d in range(1, depth)]:
        pl.semaphore_signal(barrier, inc=1, device_id={"row": target}, device_id_type=MESH)

    load_right = pltpu.make_async_copy(right_hbm, right_ref, load_sem.at[COLS])
    load_weight = pltpu.make_async_copy(weight_hbm, weight_ref, load_sem.at[COLS + 1])
    load_left = pltpu.make_async_copy(left_hbm, left_ref, load_sem.at[COLS + 2])
    loads = [load_left]
    for rel in range(COLS):
        which = col if rel == 0 else 1 - col
        loads.append(pltpu.make_async_copy(
            pair_ref.at[:, :, which, core], pair_own.at[:, rel], load_sem.at[rel]))
    for copy in [load_right, load_weight] + loads:
        copy.start()

    load_right.wait()
    wide = right_ref[...].astype(F32)
    rows_f32[...] = jnp.concatenate([wide, wide], axis=0).T
    low = lax.broadcasted_iota(jnp.int32, (block, lanes), 1) < n_seq
    for ep in range(HALF):
        even = rows_f32[pl.ds(2 * ep, block, stride=C), :]
        odd = rows_f32[pl.ds(2 * ep + 1, block, stride=C), :]
        gathered[0, z, ep] = jnp.where(low, even, odd).astype(BF16)

    pl.semaphore_wait(barrier, depth + 1)

    sib = []
    for rel in range(COLS):
        which = col if rel == 0 else 1 - col
        sib.append(send(pair_ref.at[:, :, which, 1 - core], pair_sib.at[:, rel],
                        sib_send.at[rel], sib_recv.at[rel], sibling))
    sib.append(send(left_hbm, left_sib, sib_send.at[2], sib_recv.at[2], sibling))
    def nearest(k):
        both = jnp.minimum(z, depth - 1 - z)
        toward = jnp.where(z < depth - 1 - z, 1, -1)
        near = z + (k + 1) // 2 * (1 if k % 2 else -1)
        return jnp.where(k <= 2 * both, near, z + toward * (k - both))

    gather_z = []
    gather_y = [send(gathered.at[0, z], gathered.at[1, z],
                     agy_send.at[z], agy_recv.at[z], across)]
    arrive_z = []
    for k in range(1, depth):
        other = nearest(k)
        gather_z.append(send(gathered.at[0, z], gathered.at[0, z],
                             agz_send.at[other], agz_recv.at[z], at_z(other)))
        arrive_z.append(send(gathered.at[0, other], gathered.at[0, other],
                             agz_send.at[other], agz_recv.at[other], at_z(other)))
        gather_y.append(send(gathered.at[0, other], gathered.at[1, other],
                             agy_send.at[other], agy_recv.at[other], across))
    for copy in gather_z:
        copy.start()
    gather_y[0].start()
    for copy in sib:
        copy.start()

    load_weight.wait()
    weight_f32[...] = weight_ref[...].astype(F32)
    for e in range(C):
        weight_perm[e * C:(e + 1) * C, :] = weight_f32[pl.ds(e, C, stride=C), :].astype(BF16)

    grads = (grad_a, grad_b, grad_c, grad_d)
    per_grad = C // GROUPS

    def project(pair, first, groups):
        taps = slice(groups[0] * per_grad * C, (groups[-1] + 1) * per_grad * C)

        def step(t, carry):
            slab = pair[pl.ds(2 * t, 2)].reshape(2 * width, -1)
            res = lax.dot_general(weight_perm[taps, :], slab, (((1,), (1,)), ((), ())),
                                  preferred_element_type=F32).astype(BF16)
            for k in range(2):
                row = pl.multiple_of(first + (2 * t + k) * C, C)
                for e in range(len(groups) * per_grad):
                    q = e % per_grad
                    grads[groups[e // per_grad]][pl.ds(row, C), q * width:(q + 1) * width] = (
                        res[e * C:(e + 1) * C, k * width:(k + 1) * width])
            return carry

        lax.fori_loop(0, block // 2, step, 0, unroll=2 if len(groups) > 1 else 4)

    reduce_y = [send(y_send.at[g], y_recv.at[g], rsy_send.at[g], rsy_recv.at[g], across)
                for g in range(GROUPS)]
    reduce_z = [
        [send(z_send.at[g, z_peer(d)], z_recv.at[g, d - 1],
              rsz_send.at[g, d - 1], rsz_recv.at[g, d - 1], at_z(z_peer(d)))
         for d in range(1, depth)]
        for g in range(GROUPS)
    ]

    def columns(g):
        res = jnp.dot(left_ref[...], grads[g][:chans, :], preferred_element_type=F32)
        res += jnp.dot(left_sib[...], grads[g][chans:, :], preferred_element_type=F32)
        for q in range(per_group):
            at = 2 * q * width
            turned = jnp.concatenate(
                [res[:, at:at + width], res[:, at + width:at + 2 * width]], axis=0).T
            where = slice(q * lanes, (q + 1) * lanes)
            column_sum[g, :, where] = turned[:span]
            y_send[g, :, where] = turned[span:].astype(BF16)

    def second(g):
        reduce_y[g].wait_recv()
        column_sum[g] += y_recv[g].astype(F32)
        for k in range(depth):
            z_send[g, k] = column_sum[g, k * block:(k + 1) * block, :].astype(BF16)
        for copy in reduce_z[g]:
            copy.start()

    def finish(g):
        acc = column_sum[g, pl.ds(pl.multiple_of(z * block, block), block), :]
        for d in range(1, depth):
            reduce_z[g][d - 1].wait_recv()
            acc += z_recv[g, d - 1].astype(F32)
        for q in range(per_group):
            ep = g * per_group + q
            tile = acc[:, q * lanes:(q + 1) * lanes] * (1.0 / n_seq)
            rows_f32[pl.ds(2 * ep, block, stride=C), :] = tile
            rows_f32[pl.ds(2 * ep + 1, block, stride=C), :] = pltpu.roll(tile, n_seq, 1)

    def rows(first):
        part = per_group * 2 * width
        acc = None
        for g in range(GROUPS):
            term = jnp.dot(grads[g][first:first + chans, :],
                           right_all[g * part:(g + 1) * part, :], preferred_element_type=F32)
            acc = term if acc is None else acc + term
        turned = acc.T
        return turned[:n_seq] + turned[n_seq:]

    for copy in loads:
        copy.wait()
    project(pair_own, 0, tuple(range(GROUPS)))
    for copy in sib:
        copy.wait_recv()
    for g in range(GROUPS):
        project(pair_sib, chans, (g,))
        columns(g)
        reduce_y[g].start()
        for k in range(1, depth):
            if max(1, 2 * k // (depth - 1)) == g:
                arrive_z[k - 1].wait_recv()
                gather_y[k].start()
        if g >= 2:
            second(g - 2)

    for copy in gather_y:
        copy.wait_recv()
    upper = lax.broadcasted_iota(jnp.int32, (width, lanes), 1) >= n_seq
    mask_odd = upper.astype(F32).astype(BF16)
    mask_even = (1.0 - upper.astype(F32)).astype(BF16)
    for ep in range(HALF):
        piece = gathered[:, :, ep].reshape(width, lanes)
        right_all[2 * ep * width:(2 * ep + 1) * width, :] = piece * mask_even
        right_all[(2 * ep + 1) * width:(2 * ep + 2) * width, :] = piece * mask_odd

    left_send[...] = rows(chans)
    exchange = send(left_send, left_recv, sib_send.at[3], sib_recv.at[3], sibling)
    exchange.start()
    second(GROUPS - 2)
    second(GROUPS - 1)
    for g in range(GROUPS // 2):
        finish(g)
    mine = rows(0)
    exchange.wait_recv()
    out[0] = ((mine + left_recv[...]) * (1.0 / n_seq)).astype(BF16)

    for g in range(GROUPS // 2, GROUPS):
        finish(g)
    out[1] = rows_f32[...].T[:n_seq].astype(BF16)

    for copy in sib + gather_z + gather_y + reduce_y + [exchange]:
        copy.wait_send()
    for group in reduce_z:
        for copy in group:
            copy.wait_send()


def per_device(n_row, left_proj, right_proj, pair_cot, out_weight):
    n_seq = left_proj.shape[0]
    block, total, p_size = pair_cot.shape
    depth = n_row // (CORES * COLS)
    span = depth * block
    width = COLS * span
    chans = block * C
    lanes = 2 * n_seq
    group_lanes = HALF // GROUPS * lanes
    pair = pair_cot.reshape(block, depth, COLS, CORES, block, p_size)
    vmem = pl.BlockSpec(memory_space=pltpu.VMEM)
    dma = pltpu.SemaphoreType.DMA
    flops = 2 * block * total * C * C * (p_size + 2 * n_seq)
    scratch = [
        pltpu.VMEM(left_proj.shape, BF16),
        pltpu.VMEM(right_proj.shape, BF16),
        pltpu.VMEM(out_weight.shape, BF16),
        pltpu.VMEM((block, COLS, depth, block, p_size), BF16),
        pltpu.VMEM((block, COLS, depth, block, p_size), BF16),
        pltpu.VMEM((n_seq, chans), BF16),
        pltpu.VMEM((C * C, p_size), F32),
        pltpu.VMEM((C * C, p_size), BF16),
        *[pltpu.VMEM((2 * chans, C // GROUPS * width), BF16)] * GROUPS,
        pltpu.VMEM((chans, lanes), F32),
        pltpu.VMEM((COLS, depth, HALF, block, lanes), BF16),
        pltpu.VMEM((C * width, lanes), BF16),
        pltpu.VMEM((GROUPS, span, group_lanes), F32),
        pltpu.VMEM((GROUPS, span, group_lanes), BF16),
        pltpu.VMEM((GROUPS, span, group_lanes), BF16),
        pltpu.VMEM((GROUPS, depth, block, group_lanes), BF16),
        pltpu.VMEM((GROUPS, depth - 1, block, group_lanes), BF16),
        pltpu.VMEM((n_seq, chans), F32),
        pltpu.VMEM((n_seq, chans), F32),
        dma((COLS + 3,)),
        dma((4,)), dma((4,)),
        dma((depth,)), dma((depth,)),
        dma((depth,)), dma((depth,)),
        dma((GROUPS,)), dma((GROUPS,)),
        dma((GROUPS, depth - 1)), dma((GROUPS, depth - 1)),
    ]
    held = sum(2 * math.prod(b.shape) if b.dtype == BF16 else 4 * math.prod(b.shape)
               for b in scratch if b.dtype in (BF16, F32))
    held += 8 * left_proj.size
    sums = pl.pallas_call(
        functools.partial(kernel, depth, n_seq, block),
        out_shape=pltpu.VMEM((2, n_seq, chans), BF16),
        in_specs=[pl.BlockSpec(memory_space=pltpu.HBM)] * 4,
        out_specs=vmem,
        scratch_shapes=scratch,
        compiler_params=pltpu.CompilerParams(
            collective_id=0, has_side_effects=True, vmem_limit_bytes=held + 4 * 1024 * 1024
        ),
        cost_estimate=pl.CostEstimate(
            flops=flops, bytes_accessed=4 * pair_cot.size, transcendentals=0
        ),
    )(*[pltpu.with_memory_space_constraint(x, pltpu.HBM)
        for x in (left_proj, right_proj, pair, out_weight)])
    return (sums[0], sums[1])


def solution(mesh):
    return jax.shard_map(
        functools.partial(per_device, mesh.shape["row"]),
        mesh=mesh,
        in_specs=(P("groups", "row"), P("groups", "row"), P(("groups", "row"), None, None), P()),
        out_specs=(P("groups", "row"), P("groups", "row")),
        check_vma=False,
    )
```

```python
import functools
import math

import jax
import jax.numpy as jnp
from jax import lax
from jax.experimental import pallas as pl
from jax.experimental.pallas import tpu as pltpu
from jax.sharding import PartitionSpec as P

C = 32
CORES = 2
COLS = 2
HALF = C // 2
GROUPS = 4
MESH = pl.DeviceIdType.MESH
F32 = jnp.float32
BF16 = jnp.bfloat16


def kernel(
    depth, n_seq, block,
    left_hbm, right_hbm, pair_ref, weight_hbm,
    out,
    left_ref, right_ref, weight_ref,
    pair_own, pair_sib, left_sib, weight_f32, weight_perm, grad_a, grad_b, grad_c, grad_d, rows_f32,
    gathered, right_all, column_sum, y_send, y_recv, z_send, z_recv,
    left_send, left_recv,
    load_sem, sib_send, sib_recv, agz_send, agz_recv, agy_send, agy_recv,
    rsy_send, rsy_recv, rsz_send, rsz_recv,
):
    me = lax.axis_index("row")
    core = lax.rem(me, CORES)
    col = lax.rem(me // CORES, COLS)
    z = me // (CORES * COLS)
    sibling = me + 1 - 2 * core
    across = me + CORES * (1 - 2 * col)
    span = depth * block
    width = COLS * span
    chans = block * C
    lanes = 2 * n_seq
    per_group = HALF // GROUPS
    group_lanes = per_group * lanes

    def z_peer(step):
        return lax.rem(z + step, depth)

    def at_z(other):
        return other * (CORES * COLS) + lax.rem(me, CORES * COLS)

    def send(src, dst, s_sem, r_sem, target):
        return pltpu.make_async_remote_copy(
            src_ref=src, dst_ref=dst, send_sem=s_sem, recv_sem=r_sem,
            device_id={"row": target}, device_id_type=MESH,
        )

    barrier = pltpu.get_barrier_semaphore()
    for target in [sibling, across] + [at_z(z_peer(d)) for d in range(1, depth)]:
        pl.semaphore_signal(barrier, inc=1, device_id={"row": target}, device_id_type=MESH)

    load_right = pltpu.make_async_copy(right_hbm, right_ref, load_sem.at[COLS])
    load_weight = pltpu.make_async_copy(weight_hbm, weight_ref, load_sem.at[COLS + 1])
    load_left = pltpu.make_async_copy(left_hbm, left_ref, load_sem.at[COLS + 2])
    loads = [load_left]
    for rel in range(COLS):
        which = col if rel == 0 else 1 - col
        loads.append(pltpu.make_async_copy(
            pair_ref.at[:, :, which, core], pair_own.at[:, rel], load_sem.at[rel]))
    for copy in [load_right, load_weight] + loads:
        copy.start()

    load_right.wait()
    wide = right_ref[...].astype(F32)
    rows_f32[...] = jnp.concatenate([wide, wide], axis=0).T
    low = lax.broadcasted_iota(jnp.int32, (block, lanes), 1) < n_seq
    for ep in range(HALF):
        even = rows_f32[pl.ds(2 * ep, block, stride=C), :]
        odd = rows_f32[pl.ds(2 * ep + 1, block, stride=C), :]
        gathered[0, z, ep] = jnp.where(low, even, odd).astype(BF16)

    pl.semaphore_wait(barrier, depth + 1)

    sib = []
    for rel in range(COLS):
        which = col if rel == 0 else 1 - col
        sib.append(send(pair_ref.at[:, :, which, 1 - core], pair_sib.at[:, rel],
                        sib_send.at[rel], sib_recv.at[rel], sibling))
    sib.append(send(left_hbm, left_sib, sib_send.at[2], sib_recv.at[2], sibling))
    def nearest(k):
        both = jnp.minimum(z, depth - 1 - z)
        toward = jnp.where(z < depth - 1 - z, 1, -1)
        near = z + (k + 1) // 2 * (1 if k % 2 else -1)
        return jnp.where(k <= 2 * both, near, z + toward * (k - both))

    gather_z = []
    gather_y = [send(gathered.at[0, z], gathered.at[1, z],
                     agy_send.at[z], agy_recv.at[z], across)]
    arrive_z = []
    for k in range(1, depth):
        other = nearest(k)
        gather_z.append(send(gathered.at[0, z], gathered.at[0, z],
                             agz_send.at[other], agz_recv.at[z], at_z(other)))
        arrive_z.append(send(gathered.at[0, other], gathered.at[0, other],
                             agz_send.at[other], agz_recv.at[other], at_z(other)))
        gather_y.append(send(gathered.at[0, other], gathered.at[1, other],
                             agy_send.at[other], agy_recv.at[other], across))
    for copy in gather_z:
        copy.start()
    gather_y[0].start()
    for copy in sib:
        copy.start()

    load_weight.wait()
    weight_f32[...] = weight_ref[...].astype(F32)
    for e in range(C):
        weight_perm[e * C:(e + 1) * C, :] = weight_f32[pl.ds(e, C, stride=C), :].astype(BF16)

    grads = (grad_a, grad_b, grad_c, grad_d)
    per_grad = C // GROUPS

    def project(pair, first, groups):
        taps = slice(groups[0] * per_grad * C, (groups[-1] + 1) * per_grad * C)

        def step(t, carry):
            slab = pair[pl.ds(2 * t, 2)].reshape(2 * width, -1)
            res = lax.dot_general(weight_perm[taps, :], slab, (((1,), (1,)), ((), ())),
                                  preferred_element_type=F32).astype(BF16)
            for k in range(2):
                row = pl.multiple_of(first + (2 * t + k) * C, C)
                for e in range(len(groups) * per_grad):
                    q = e % per_grad
                    grads[groups[e // per_grad]][pl.ds(row, C), q * width:(q + 1) * width] = (
                        res[e * C:(e + 1) * C, k * width:(k + 1) * width])
            return carry

        lax.fori_loop(0, block // 2, step, 0, unroll=2 if len(groups) > 1 else 4)

    reduce_y = [send(y_send.at[g], y_recv.at[g], rsy_send.at[g], rsy_recv.at[g], across)
                for g in range(GROUPS)]
    reduce_z = [
        [send(z_send.at[g, z_peer(d)], z_recv.at[g, d - 1],
              rsz_send.at[g, d - 1], rsz_recv.at[g, d - 1], at_z(z_peer(d)))
         for d in range(1, depth)]
        for g in range(GROUPS)
    ]

    def columns(g):
        res = jnp.dot(left_ref[...], grads[g][:chans, :], preferred_element_type=F32)
        res += jnp.dot(left_sib[...], grads[g][chans:, :], preferred_element_type=F32)
        for q in range(per_group):
            at = 2 * q * width
            turned = jnp.concatenate(
                [res[:, at:at + width], res[:, at + width:at + 2 * width]], axis=0).T
            where = slice(q * lanes, (q + 1) * lanes)
            column_sum[g, :, where] = turned[:span]
            y_send[g, :, where] = turned[span:].astype(BF16)

    def second(g):
        reduce_y[g].wait_recv()
        column_sum[g] += y_recv[g].astype(F32)
        for k in range(depth):
            z_send[g, k] = column_sum[g, k * block:(k + 1) * block, :].astype(BF16)
        for copy in reduce_z[g]:
            copy.start()

    def finish(g):
        acc = column_sum[g, pl.ds(pl.multiple_of(z * block, block), block), :]
        for d in range(1, depth):
            reduce_z[g][d - 1].wait_recv()
            acc += z_recv[g, d - 1].astype(F32)
        for q in range(per_group):
            ep = g * per_group + q
            tile = acc[:, q * lanes:(q + 1) * lanes] * (1.0 / n_seq)
            rows_f32[pl.ds(2 * ep, block, stride=C), :] = tile
            rows_f32[pl.ds(2 * ep + 1, block, stride=C), :] = pltpu.roll(tile, n_seq, 1)

    def rows(first):
        part = per_group * 2 * width
        acc = None
        for g in range(GROUPS):
            term = jnp.dot(grads[g][first:first + chans, :],
                           right_all[g * part:(g + 1) * part, :], preferred_element_type=F32)
            acc = term if acc is None else acc + term
        turned = acc.T
        return turned[:n_seq] + turned[n_seq:]

    for copy in loads:
        copy.wait()
    project(pair_own, 0, tuple(range(GROUPS)))
    for copy in sib:
        copy.wait_recv()
    for g in range(GROUPS):
        project(pair_sib, chans, (g,))
        columns(g)
        reduce_y[g].start()
        for k in range(1, depth):
            if g == 0:
                arrive_z[k - 1].wait_recv()
                gather_y[k].start()
        if g >= 2:
            second(g - 2)

    for copy in gather_y:
        copy.wait_recv()
    upper = lax.broadcasted_iota(jnp.int32, (width, lanes), 1) >= n_seq
    mask_odd = upper.astype(F32).astype(BF16)
    mask_even = (1.0 - upper.astype(F32)).astype(BF16)
    for ep in range(HALF):
        piece = gathered[:, :, ep].reshape(width, lanes)
        right_all[2 * ep * width:(2 * ep + 1) * width, :] = piece * mask_even
        right_all[(2 * ep + 1) * width:(2 * ep + 2) * width, :] = piece * mask_odd

    left_send[...] = rows(chans)
    exchange = send(left_send, left_recv, sib_send.at[3], sib_recv.at[3], sibling)
    exchange.start()
    second(GROUPS - 2)
    second(GROUPS - 1)
    for g in range(GROUPS // 2):
        finish(g)
    mine = rows(0)
    exchange.wait_recv()
    out[0] = ((mine + left_recv[...]) * (1.0 / n_seq)).astype(BF16)

    for g in range(GROUPS // 2, GROUPS):
        finish(g)
    out[1] = rows_f32[...].T[:n_seq].astype(BF16)

    for copy in sib + gather_z + gather_y + reduce_y + [exchange]:
        copy.wait_send()
    for group in reduce_z:
        for copy in group:
            copy.wait_send()


def per_device(n_row, left_proj, right_proj, pair_cot, out_weight):
    n_seq = left_proj.shape[0]
    block, total, p_size = pair_cot.shape
    depth = n_row // (CORES * COLS)
    span = depth * block
    width = COLS * span
    chans = block * C
    lanes = 2 * n_seq
    group_lanes = HALF // GROUPS * lanes
    pair = pair_cot.reshape(block, depth, COLS, CORES, block, p_size)
    vmem = pl.BlockSpec(memory_space=pltpu.VMEM)
    dma = pltpu.SemaphoreType.DMA
    flops = 2 * block * total * C * C * (p_size + 2 * n_seq)
    scratch = [
        pltpu.VMEM(left_proj.shape, BF16),
        pltpu.VMEM(right_proj.shape, BF16),
        pltpu.VMEM(out_weight.shape, BF16),
        pltpu.VMEM((block, COLS, depth, block, p_size), BF16),
        pltpu.VMEM((block, COLS, depth, block, p_size), BF16),
        pltpu.VMEM((n_seq, chans), BF16),
        pltpu.VMEM((C * C, p_size), F32),
        pltpu.VMEM((C * C, p_size), BF16),
        *[pltpu.VMEM((2 * chans, C // GROUPS * width), BF16)] * GROUPS,
        pltpu.VMEM((chans, lanes), F32),
        pltpu.VMEM((COLS, depth, HALF, block, lanes), BF16),
        pltpu.VMEM((C * width, lanes), BF16),
        pltpu.VMEM((GROUPS, span, group_lanes), F32),
        pltpu.VMEM((GROUPS, span, group_lanes), BF16),
        pltpu.VMEM((GROUPS, span, group_lanes), BF16),
        pltpu.VMEM((GROUPS, depth, block, group_lanes), BF16),
        pltpu.VMEM((GROUPS, depth - 1, block, group_lanes), BF16),
        pltpu.VMEM((n_seq, chans), F32),
        pltpu.VMEM((n_seq, chans), F32),
        dma((COLS + 3,)),
        dma((4,)), dma((4,)),
        dma((depth,)), dma((depth,)),
        dma((depth,)), dma((depth,)),
        dma((GROUPS,)), dma((GROUPS,)),
        dma((GROUPS, depth - 1)), dma((GROUPS, depth - 1)),
    ]
    held = sum(2 * math.prod(b.shape) if b.dtype == BF16 else 4 * math.prod(b.shape)
               for b in scratch if b.dtype in (BF16, F32))
    held += 8 * left_proj.size
    sums = pl.pallas_call(
        functools.partial(kernel, depth, n_seq, block),
        out_shape=pltpu.VMEM((2, n_seq, chans), BF16),
        in_specs=[pl.BlockSpec(memory_space=pltpu.HBM)] * 4,
        out_specs=vmem,
        scratch_shapes=scratch,
        compiler_params=pltpu.CompilerParams(
            collective_id=0, has_side_effects=True, vmem_limit_bytes=held + 4 * 1024 * 1024
        ),
        cost_estimate=pl.CostEstimate(
            flops=flops, bytes_accessed=4 * pair_cot.size, transcendentals=0
        ),
    )(*[pltpu.with_memory_space_constraint(x, pltpu.HBM)
        for x in (left_proj, right_proj, pair, out_weight)])
    return (sums[0], sums[1])


def solution(mesh):
    return jax.shard_map(
        functools.partial(per_device, mesh.shape["row"]),
        mesh=mesh,
        in_specs=(P("groups", "row"), P("groups", "row"), P(("groups", "row"), None, None), P()),
        out_specs=(P("groups", "row"), P("groups", "row")),
        check_vma=False,
    )
```
